512 devices in a mesh: gz: 64 (over z, y_hi, core), xy: 8 (over y_lo, x).
Axes of the slice: x: 4, y: 4 (y_hi: 2, y_lo: 2; y = y_hi * 2 + y_lo), z: 16, core: 2. Of those that a mesh axis runs over, the one named last changes fastest.
Arguments:
- patch_features: bfloat16 [16, 640, 144, 128], P(None, 'gz', 'xy'), may hold values from -6 to 6
- conv1_weight: bfloat16 [16, 16, 3, 3, 3], replicated, may hold values from -0.3125 to 0.3125
- conv1_bias: float32 [16], replicated, may hold values from -3 to 3
- conv2_weight: bfloat16 [16, 16, 3, 3, 3], replicated, may hold values from -0.3125 to 0.3125
- conv2_bias: float32 [16], replicated, may hold values from -3 to 3
- head_weight: bfloat16 [16], replicated, may hold values from -3 to 3
- tissue_mask: int32 [512, 128, 128], P('gz', 'xy'), may hold values 0 or 1
Outputs:
- probability: float32 [512, 128, 128], P('gz', 'xy')
- vesselness: float32 [512, 128, 128], P('gz', 'xy')
The draws below stay inside these ranges and needn't reach their ends.
All inputs are finite; a program needn't handle non-finite values. No bound on the sum of `tissue_mask` on one device may be relied on, other than what follows from the above.
Results may differ from the reference program's by a relative error of at most 0.0025.
The reference program's roundings to bfloat16 on the way count: a program that leaves them out, or rounds other values in their place, can miss the bound.
Values sent between devices are 32-bit elements; how exact they have to be, the bound alone decides.
No kernel may reach another device: no remote copies, remote signals or barrier semaphores. Data moves between devices by JAX's collectives and lax.ppermute only.
A program may use at most 128 MiB of HBM per device.

```python
import jax
import jax.numpy as jnp
from jax import lax

CHANNELS = 16
CZ = 8
CX = 16
YC = 128
MARGIN = 1
RIM = 8
NZ = 512
NX = 128
N_GZ = 64
N_XY = 8


def plant(drawn, stream_key, least, high):
    spot = [jax.random.randint(jax.random.fold_in(stream_key, axis), (), 0, length) for axis, length in enumerate(drawn.shape)]
    widest = drawn.shape.index(max(drawn.shape))
    next_to = spot[:widest] + [(spot[widest] + 1) % drawn.shape[widest]] + spot[widest + 1:]
    return drawn.at[tuple(spot)].set(least).at[tuple(next_to)].set(high)


def block_scale(stream_key, shape, split, smallest, largest):
    def one(axis_at, parts):
        steps = jax.random.uniform(jax.random.fold_in(jax.random.fold_in(stream_key, 6), axis_at), (parts,), jnp.float32, smallest / len(split), largest / len(split))
        return jnp.repeat(jnp.exp(steps), shape[axis_at] // parts).reshape((-1,) + (1,) * (len(shape) - axis_at - 1))

    level = one(*split[0])
    for cut in split[1:]:
        level = level * one(*cut)
    return level


def scatter_about(key, extent, scale, most, cuts=(), dtype=jnp.bfloat16):
    values = scale * jax.random.normal(key, extent, jnp.float32)
    if cuts:
        values = values * block_scale(key, extent, cuts, -0.22, 0.18)
    return jnp.clip(values, -most, most).astype(dtype)


def setup_inputs(seed: int = 0) -> dict:
    splits = jax.random.split(jax.random.key(seed), 8)
    return {
        "patch_features": scatter_about(splits[0], (CHANNELS, (CZ + 2 * MARGIN) * N_GZ, (CX + 2 * MARGIN) * N_XY, YC), 1.0, 6.0, ((1, 64), (2, 8))),
        "conv1_weight": scatter_about(splits[1], (CHANNELS, CHANNELS, 3, 3, 3), (CHANNELS * 27) ** -0.5, 0.3125),
        "conv1_bias": scatter_about(splits[2], (CHANNELS,), 0.5, 3.0, (), jnp.float32),
        "conv2_weight": scatter_about(splits[3], (CHANNELS, CHANNELS, 3, 3, 3), (CHANNELS * 27) ** -0.5, 0.3125),
        "conv2_bias": scatter_about(splits[4], (CHANNELS,), 0.5, 3.0, (), jnp.float32),
        "head_weight": scatter_about(splits[5], (CHANNELS,), 0.6, 3.0),
        "tissue_mask": plant((jax.random.randint(splits[6], (NZ, NX, YC), 0, 4) < 3).astype(jnp.int32), jax.random.fold_in(splits[6], 1), 0, 1),
    }


CONV_DIMS = ("NCDHW", "OIDHW", "NCDHW")
VESSEL_GAIN = 4.0
TUBE_FLOOR = 0.01


def window(size):
    position = jnp.arange(size).astype(jnp.float32)
    return jnp.exp(-0.5 * ((position - (size - 1) / 2.0) / (size / 4.0)) ** 2)


def conv_layer(inputs, weight, bias):
    summed = lax.conv_general_dilated(inputs[None].astype(jnp.float32), weight.astype(jnp.float32), (1, 1, 1), "SAME", dimension_numbers=CONV_DIMS, precision=lax.Precision.HIGHEST)[0]
    return jax.nn.relu(summed + bias[:, None, None, None]).astype(jnp.bfloat16)


def kernel_taps(radius, degree):
    spread = radius / 3.0
    offsets = jnp.arange(-radius, radius + 1).astype(jnp.float32)
    gaussian = jnp.exp(-offsets * offsets / (2.0 * spread * spread))
    gaussian = gaussian / jnp.sum(gaussian)
    if degree == 1:
        return -offsets / (spread * spread) * gaussian
    if degree == 2:
        return (offsets * offsets / spread ** 4 - 1.0 / (spread * spread)) * gaussian
    return gaussian


def smooth(volume, axis, radius, degree):
    weights_line = kernel_taps(radius, degree)
    length = volume.shape[axis]
    widths = [(0, 0), (0, 0), (0, 0)]
    widths[axis] = (radius, radius)
    padded = jnp.pad(volume, widths)
    result = jnp.zeros_like(volume)
    for tap in range(2 * radius + 1):
        result = result + weights_line[tap] * lax.slice_in_dim(padded, 2 * radius - tap, 2 * radius - tap + length, axis=axis)
    return result


def tubeness(hzz, hxx, hyy, hzx, hzy, hxy):
    first_inv = hzz + hxx + hyy
    second_inv = hzz * hxx + hzz * hyy + hxx * hyy - hzx * hzx - hzy * hzy - hxy * hxy
    third_inv = hzz * (hxx * hyy - hxy * hxy) - hzx * (hzx * hyy - hxy * hzy) + hzy * (hzx * hxy - hxx * hzy)
    positive = jax.nn.relu(second_inv)
    return jax.nn.relu(-first_inv) * positive / (positive + jnp.cbrt(third_inv * third_inv) + TUBE_FLOOR)


def hessian_tube(volume, radius):
    scale_sq = (radius / 3.0) ** 2
    along_z = [smooth(volume, 0, radius, degree) for degree in range(3)]
    flat_flat = smooth(along_z[0], 1, radius, 0)
    flat_slope = smooth(along_z[0], 1, radius, 1)
    flat_curve = smooth(along_z[0], 1, radius, 2)
    slope_flat = smooth(along_z[1], 1, radius, 0)
    slope_slope = smooth(along_z[1], 1, radius, 1)
    curve_flat = smooth(along_z[2], 1, radius, 0)
    hzz = scale_sq * smooth(curve_flat, 2, radius, 0)
    hxx = scale_sq * smooth(flat_curve, 2, radius, 0)
    hyy = scale_sq * smooth(flat_flat, 2, radius, 2)
    hzx = scale_sq * smooth(slope_slope, 2, radius, 0)
    hzy = scale_sq * smooth(slope_flat, 2, radius, 1)
    hxy = scale_sq * smooth(flat_slope, 2, radius, 1)
    return tubeness(hzz, hxx, hyy, hzx, hzy, hxy)


def reference(patch_features, conv1_weight, conv1_bias, conv2_weight, conv2_bias, head_weight, tissue_mask):
    span_z = CZ + 2 * MARGIN
    span_x = CX + 2 * MARGIN
    count = N_GZ * N_XY
    patches = patch_features.reshape(CHANNELS, N_GZ, span_z, N_XY, span_x, YC).transpose(1, 3, 0, 2, 4, 5).reshape(count, CHANNELS, span_z, span_x, YC)

    def decode(features):
        hidden = conv_layer(features, conv1_weight, conv1_bias)
        hidden = conv_layer(hidden, conv2_weight, conv2_bias)
        return jnp.einsum("c,czxy->zxy", head_weight.astype(jnp.float32), hidden.astype(jnp.float32), precision=lax.Precision.HIGHEST)

    logits = lax.map(decode, patches)
    weights = window(span_z)[:, None, None] * window(span_x)[None, :, None]

    def place(patch_index, canvas):
        slab_idx = (patch_index // N_XY).astype(jnp.int32)
        block_idx = (patch_index % N_XY).astype(jnp.int32)
        start_z = slab_idx * CZ
        start_x = block_idx * CX
        zero_idx = jnp.zeros((), jnp.int32)
        current = lax.dynamic_slice(canvas, (start_z, start_x, zero_idx), (span_z, span_x, YC))
        return lax.dynamic_update_slice(canvas, current + logits[patch_index] * weights, (start_z, start_x, zero_idx))

    canvas = lax.fori_loop(0, count, place, jnp.zeros((NZ + 2 * MARGIN, NX + 2 * MARGIN, YC), jnp.float32))
    blended_sum = canvas[MARGIN:MARGIN + NZ, MARGIN:MARGIN + NX]

    def cover(core, span, count_axis):
        positions = (jnp.arange(count_axis)[:, None] * core + jnp.arange(span)[None, :]).reshape(-1).astype(jnp.int32)
        line = jnp.zeros((core * count_axis + 2 * MARGIN,), jnp.float32).at[positions].add(jnp.tile(window(span), count_axis))
        return line[MARGIN:MARGIN + core * count_axis]

    coverage = cover(CZ, span_z, N_GZ)[:, None, None] * cover(CX, span_x, N_XY)[None, :, None]
    probability = jax.nn.sigmoid(blended_sum / coverage)
    vessel_sum = jnp.zeros_like(probability)
    for radius in (RIM // 4, RIM // 2, RIM):
        vessel_sum = vessel_sum + hessian_tube(probability, radius)
    vesselness = VESSEL_GAIN * tissue_mask.astype(jnp.float32) * vessel_sum
    return probability, vesselness
```

```python
import jax
import jax.numpy as jnp
import numpy as np
from jax import lax
from jax.experimental import pallas as pl
from jax.experimental.pallas import tpu as pltpu
from jax.sharding import PartitionSpec as P

CHANNELS = 16
CZ = 8
CX = 16
YC = 128
MARGIN = 1
RIM = 8
SPAN_Z = CZ + 2 * MARGIN
SPAN_X = CX + 2 * MARGIN
HALF = SPAN_X // 2
ROWS = SPAN_Z * CHANNELS
SLOT = 512
RADII = (RIM // 4, RIM // 2, RIM)
VESSEL_GAIN = 4.0
TUBE_FLOOR = 0.01
VMEM_LIMIT = 40 * 1024 * 1024


def window(size):
    position = np.arange(size, dtype=np.float64)
    return np.exp(-0.5 * ((position - (size - 1) / 2.0) / (size / 4.0)) ** 2)


WINDOW_Z = window(SPAN_Z)
WINDOW_X = window(SPAN_X)


def taps(radius, degree):
    spread = radius / 3.0
    offsets = np.arange(-radius, radius + 1, dtype=np.float64)
    gaussian = np.exp(-offsets * offsets / (2.0 * spread * spread))
    gaussian = gaussian / gaussian.sum()
    if degree == 1:
        return -offsets / spread**2 * gaussian
    if degree == 2:
        return (offsets**2 / spread**4 - 1.0 / spread**2) * gaussian
    return gaussian


def band(out_len, in_len, offset, radius, degree):
    weights = taps(radius, degree)
    distance = np.arange(out_len)[:, None] + offset - np.arange(in_len)[None, :]
    inside = np.abs(distance) <= radius
    return np.where(inside, weights[np.clip(distance, -radius, radius) + radius], 0.0)


def split_terms(matrix):
    whole = matrix.astype(np.float32)
    upper = whole.astype(jnp.bfloat16)
    lower = (whole - upper.astype(np.float32)).astype(jnp.bfloat16)
    return upper, lower


def filter_constants():
    x_upper, x_lower, y_all = [], [], []
    for radius in RADII:
        blocks = [
            np.kron(np.eye(CZ), band(CX, CX + 2 * RIM, RIM, radius, degree)) for degree in range(3)
        ]
        upper, lower = split_terms(np.concatenate(blocks, axis=0))
        x_upper.append(upper)
        x_lower.append(lower)
        for degree in range(3):
            scaled = (radius / 3.0) ** 2 * band(YC, YC, 0, radius, degree).T
            upper, lower = split_terms(scaled)
            top = np.concatenate([upper, lower], axis=1)
            bottom = np.concatenate([upper, np.zeros_like(lower)], axis=1)
            y_all.append(np.concatenate([top, bottom], axis=0))
    return np.stack(x_upper), np.stack(x_lower), np.stack(y_all)


def iota(shape, dim):
    return lax.broadcasted_iota(jnp.int32, shape, dim)


def y_neighbours(values):
    lane = iota(values.shape, 1)
    before = jnp.where(lane == 0, 0.0, pltpu.roll(values, 1, 1))
    after = jnp.where(lane == YC - 1, 0.0, pltpu.roll(values, YC - 1, 1))
    return (before, values, after)


def store_column(slots_ref, slot, half, three):
    lanes = pl.ds(half * YC, YC)
    for dy in range(3):
        slots_ref[pl.ds(slot * SLOT + dy * ROWS, ROWS), lanes] = three[dy]


def expand_weight(weight_ref, wide_ref):
    lane = iota((CHANNELS, SLOT), 1)
    group = (lane >= ROWS).astype(jnp.int32) + (lane >= 2 * ROWS).astype(jnp.int32) + (
        lane >= 3 * ROWS
    ).astype(jnp.int32)
    row = iota((CHANNELS, SLOT), 0)
    same = (lane & (CHANNELS - 1)) == row
    spread = jnp.zeros((9 * CHANNELS, SLOT), jnp.float32)
    for dy in range(3):
        pick = jnp.where(same & (group == dy), 1.0, 0.0).astype(jnp.bfloat16)
        part = weight_ref[:, :, dy].reshape(9 * CHANNELS, CHANNELS)
        spread = spread + jnp.dot(part, pick, preferred_element_type=jnp.float32)
    plane = (lane - group * ROWS) >> 4
    for dx in range(3):
        three = [
            spread[(dz * 3 + dx) * CHANNELS : (dz * 3 + dx + 1) * CHANNELS] for dz in range(3)
        ]
        for z in range(SPAN_Z):
            rows = jnp.where(
                plane == z - 1,
                three[0],
                jnp.where(plane == z, three[1], jnp.where(plane == z + 1, three[2], 0.0)),
            )
            wide_ref[z * CHANNELS : (z + 1) * CHANNELS, dx * SLOT : (dx + 1) * SLOT] = rows.astype(
                jnp.bfloat16
            )


def column_of(row_ref):
    eye = iota((CHANNELS, CHANNELS), 0) == iota((CHANNELS, CHANNELS), 1)
    return jnp.sum(jnp.where(eye, row_ref[...], 0.0), axis=1, keepdims=True)


def decoder_kernel(
    features_ref,
    weight1_ref,
    bias1_ref,
    weight2_ref,
    bias2_ref,
    head_ref,
    patch_ref,
    low_ref,
    high_ref,
    first_ref,
    second_ref,
    wide1_ref,
    wide2_ref,
):
    expand_weight(weight1_ref, wide1_ref)
    expand_weight(weight2_ref, wide2_ref)
    for ref in (first_ref, second_ref):
        ref[0:SLOT, 0:YC] = jnp.zeros((SLOT, YC), jnp.bfloat16)
        ref[(HALF + 1) * SLOT :, YC:] = jnp.zeros((SLOT, YC), jnp.bfloat16)
        for slot in range(HALF + 2):
            ref[slot * SLOT + 3 * ROWS : (slot + 1) * SLOT, :] = jnp.zeros(
                (SLOT - 3 * ROWS, 2 * YC), jnp.bfloat16
            )
    for x in range(SPAN_X):
        column = features_ref[:, x].reshape(ROWS, YC).astype(jnp.float32)
        three = [v.astype(jnp.bfloat16) for v in y_neighbours(column)]
        if x <= HALF:
            store_column(first_ref, x + 1, 0, three)
        if x >= HALF - 1:
            store_column(first_ref, x - HALF + 1, 1, three)

    def layer(wide_ref, slots_ref, bias, step):
        summed = jnp.dot(
            wide_ref[...],
            slots_ref[step * SLOT : (step + 3) * SLOT, :],
            preferred_element_type=jnp.float32,
        )
        shaped = summed.reshape(SPAN_Z, CHANNELS, 2 * YC) + bias[None]
        return jnp.maximum(shaped, 0.0).reshape(ROWS, 2 * YC)

    bias1 = column_of(bias1_ref)
    for step in range(HALF):
        hidden = layer(wide1_ref, first_ref, bias1, step)
        for half in range(2):
            part = hidden[:, half * YC : (half + 1) * YC]
            three = [v.astype(jnp.bfloat16) for v in y_neighbours(part)]
            store_column(second_ref, step + 1, half, three)
            if half == 0 and step == HALF - 1:
                store_column(second_ref, 0, 1, three)
            if half == 1 and step == 0:
                store_column(second_ref, HALF + 1, 0, three)

    bias2 = column_of(bias2_ref)
    repeat = ((iota((CHANNELS, ROWS), 1) & (CHANNELS - 1)) == iota((CHANNELS, ROWS), 0)).astype(
        jnp.float32
    )
    head_lanes = jnp.sum(
        repeat * column_of(head_ref), axis=0, keepdims=True
    )
    head = jnp.where(
        (iota((16, ROWS), 1) >> 4) == iota((16, ROWS), 0), head_lanes, 0.0
    ).astype(jnp.bfloat16)
    place = iota((16, YC), 0).astype(jnp.float32)
    centred = (place - (SPAN_Z - 1) / 2.0) / (SPAN_Z / 4.0)
    weight_z = jnp.exp(-0.5 * centred * centred)
    low_ref[16:24] = jnp.zeros((8, YC), jnp.float32)
    high_ref[16:24] = jnp.zeros((8, YC), jnp.float32)
    for step in range(HALF):
        hidden = layer(wide2_ref, second_ref, bias2, step).astype(jnp.bfloat16)
        logits = jnp.dot(head, hidden, preferred_element_type=jnp.float32)
        for half in range(2):
            x = step + half * HALF
            weighted = logits[:, half * YC : (half + 1) * YC] * (weight_z * float(WINDOW_X[x]))
            if x == 0 or x == SPAN_X - 1:
                side = 0 if x == 0 else 1
                patch_ref[160 + side * 16 : 176 + side * 16, :] = weighted
                row = 16 + side
            else:
                patch_ref[pl.ds(x - 1, SPAN_Z, stride=CX), :] = weighted[:SPAN_Z]
                row = x - 1
            low_ref[row : row + 1, :] = weighted[0:1]
            high_ref[row : row + 1, :] = weighted[SPAN_Z - 1 : SPAN_Z]


def slab_kernel(below_ref, own_ref, above_ref, far_below_ref, far_above_ref, left_ref, right_ref):
    refs = (below_ref, own_ref, above_ref)
    row = iota((CZ, YC), 0)
    for block in range(3):
        ref = refs[block]
        for i in range(CZ):
            value = ref[(i + 1) * CX : (i + 2) * CX, :]
            if i == 0:
                if block == 0:
                    value = value + far_below_ref[0:CX]
                else:
                    value = value + refs[block - 1][9 * CX : 10 * CX, :]
            if i == CZ - 1:
                if block == 2:
                    value = value + far_above_ref[0:CX]
                else:
                    value = value + refs[block + 1][0:CX, :]
            z = block * CZ + i
            left_ref[z * 8 : (z + 1) * 8, :] = value[:8]
            right_ref[z * 8 : (z + 1) * 8, :] = value[8:]
        for side, out_ref in enumerate((left_ref, right_ref)):
            base = 160 + side * 16
            value = ref[base + 1 : base + 9, :]
            if block == 0:
                lower = far_below_ref[16 + side : 17 + side]
            else:
                lower = refs[block - 1][base + 9 : base + 10, :]
            if block == 2:
                upper = far_above_ref[16 + side : 17 + side]
            else:
                upper = refs[block + 1][base : base + 1, :]
            value = value + jnp.where(row == 0, lower, 0.0) + jnp.where(row == CZ - 1, upper, 0.0)
            out_ref[192 + block * 8 : 200 + block * 8, :] = value


def two_terms(values):
    upper = values.astype(jnp.bfloat16)
    lower = (values - upper.astype(jnp.float32)).astype(jnp.bfloat16)
    return upper, lower


def vessel_kernel(
    place_ref,
    left_ref,
    right_ref,
    from_left_ref,
    from_right_ref,
    tissue_ref,
    x_upper_ref,
    x_lower_ref,
    y_ref,
    probability_ref,
    vessel_ref,
    extended_ref,
    along_z_ref,
):
    at_z, count_z, at_x, count_x = (place_ref[k] for k in range(4))
    sub = iota((8, YC), 0)

    def inverse_x(first, edge, edge_row, present):
        cover = jnp.zeros((8, YC), jnp.float32)
        for j in range(8):
            cover = jnp.where(sub == j, float(WINDOW_X[first + j + 1]), cover)
        extra = jnp.where(present, float(edge), 0.0)
        return 1.0 / (cover + jnp.where(sub == edge_row, extra, 0.0))

    wx_last, wx_first = WINDOW_X[SPAN_X - 1], WINDOW_X[0]
    yes = at_x >= 0
    inverse = [
        inverse_x(8, wx_first, 7, yes),
        inverse_x(0, wx_last, 0, at_x > 0),
        inverse_x(8, wx_first, 7, at_x < count_x - 1),
        inverse_x(0, wx_last, 0, yes),
    ]
    wz_last, wz_first = WINDOW_Z[SPAN_Z - 1], WINDOW_Z[0]
    lower_there = (at_z > 1, at_z > 0, yes)
    upper_there = (yes, at_z < count_z - 1, at_z < count_z - 2)
    inside_x = (at_x > 0, yes, yes, at_x < count_x - 1)
    inside_z = (at_z > 0, yes, at_z < count_z - 1)
    keep_x = [jnp.where(flag, 1.0, 0.0) for flag in inside_x]
    keep_z = [jnp.where(flag, 1.0, 0.0) for flag in inside_z]
    for z in range(3 * CZ):
        block, i = divmod(z, CZ)
        plain = WINDOW_Z[i + 1]
        scale = float(1.0 / plain)
        if i == 0:
            scale = jnp.where(lower_there[block], float(1.0 / (plain + wz_last)), scale)
        if i == CZ - 1:
            scale = jnp.where(upper_there[block], float(1.0 / (plain + wz_first)), scale)
        rows = slice(z * 8, (z + 1) * 8)
        edge = slice(192 + z, 193 + z)
        sums = (
            from_left_ref[rows, :] + jnp.where(sub == 7, left_ref[edge, :], 0.0),
            left_ref[rows, :] + jnp.where(sub == 0, from_left_ref[edge, :], 0.0),
            right_ref[rows, :] + jnp.where(sub == 7, from_right_ref[edge, :], 0.0),
            from_right_ref[rows, :] + jnp.where(sub == 0, right_ref[edge, :], 0.0),
        )
        for k in range(4):
            value = 1.0 / (1.0 + jnp.exp(-(sums[k] * (inverse[k] * scale))))
            if block == 1 and k in (1, 2):
                at = i * CX + (k - 1) * 8
                probability_ref[at : at + 8, :] = value
            else:
                value = value * (keep_x[k] * keep_z[block])
            extended_ref[z * 32 + k * 8 : z * 32 + k * 8 + 8, :] = value

    weights = [[taps(radius, degree) for degree in range(3)] for radius in RADII]

    def one_plane(i, carry):
        def plane(offset):
            return extended_ref[pl.ds(pl.multiple_of((i + RIM + offset) * 32, 32), 32), :]

        centre = plane(0)
        results = {}
        for n, radius in enumerate(RADII):
            for degree in (0, 2):
                results[n, degree] = centre * float(weights[n][degree][radius])
        for k in range(1, RIM + 1):
            before, after = plane(-k), plane(k)
            both, change = before + after, before - after
            for n, radius in enumerate(RADII):
                if k > radius:
                    continue
                for degree in range(3):
                    term = (change if degree == 1 else both) * float(weights[n][degree][radius + k])
                    if (n, degree) in results:
                        results[n, degree] = results[n, degree] + term
                    else:
                        results[n, degree] = term
        for n in range(3):
            for degree in range(3):
                upper, lower = two_terms(results[n, degree])
                rows = pl.ds(pl.multiple_of((n * 3 + degree) * 256 + i * 32, 32), 32)
                along_z_ref[rows, 0:YC] = upper
                along_z_ref[rows, YC : 2 * YC] = lower
        return carry

    lax.fori_loop(0, CZ, one_plane, 0)

    total = jnp.zeros((CZ * CX, YC), jnp.float32)
    for n in range(3):
        after_x = {}
        for degree in range(3):
            count = (3 - degree) * 128
            data = along_z_ref[(n * 3 + degree) * 256 : (n * 3 + degree + 1) * 256, :]
            wide = jnp.dot(x_upper_ref[n, :count], data, preferred_element_type=jnp.float32)
            narrow = jnp.dot(
                x_lower_ref[n, :count], data[:, :YC], preferred_element_type=jnp.float32
            )
            summed = wide[:, :YC] + wide[:, YC:] + narrow
            for other in range(3 - degree):
                after_x[degree, other] = summed[other * 128 : (other + 1) * 128]

        def along_y(degree, keys):
            stacked = jnp.concatenate([after_x[key] for key in keys], axis=0)
            pair = jnp.concatenate(two_terms(stacked), axis=1)
            wide = jnp.dot(pair, y_ref[n * 3 + degree], preferred_element_type=jnp.float32)
            summed = wide[:, :YC] + wide[:, YC:]
            return [summed[at * 128 : (at + 1) * 128] for at in range(len(keys))]

        hzz, hxx, hzx = along_y(0, ((2, 0), (0, 2), (1, 1)))
        hzy, hxy = along_y(1, ((1, 0), (0, 1)))
        (hyy,) = along_y(2, ((0, 0),))
        first_inv = hzz + hxx + hyy
        second_inv = hzz * hxx + hzz * hyy + hxx * hyy - hzx * hzx - hzy * hzy - hxy * hxy
        third_inv = (
            hzz * (hxx * hyy - hxy * hxy)
            - hzx * (hzx * hyy - hxy * hzy)
            + hzy * (hzx * hxy - hxx * hzy)
        )
        positive = jnp.maximum(second_inv, 0.0)
        size = jnp.abs(third_inv)
        root = jnp.where(size > 0.0, jnp.exp(jnp.log(size) * (2.0 / 3.0)), 0.0)
        total = total + jnp.maximum(-first_inv, 0.0) * positive / (positive + root + TUBE_FLOOR)
    vessel_ref[...] = VESSEL_GAIN * tissue_ref[...].astype(jnp.float32) * total


def from_behind(block, axis, distance):
    devices = range(lax.axis_size(axis))
    route = [(i - distance, i) for i in devices if i - distance in devices]
    return lax.ppermute(block, axis, route)


def whole(count):
    return [pl.BlockSpec(memory_space=pltpu.VMEM)] * count


def on_device(
    patch_features, conv1_weight, conv1_bias, conv2_weight, conv2_bias, head_weight, tissue_mask
):
    f32 = jnp.float32
    params = pltpu.CompilerParams(vmem_limit_bytes=VMEM_LIMIT)
    patch, low, high = pl.pallas_call(
        decoder_kernel,
        out_shape=(
            jax.ShapeDtypeStruct((192, YC), f32),
            jax.ShapeDtypeStruct((24, YC), f32),
            jax.ShapeDtypeStruct((24, YC), f32),
        ),
        in_specs=whole(6),
        out_specs=tuple(whole(3)),
        scratch_shapes=[
            pltpu.VMEM(((HALF + 2) * SLOT, 2 * YC), jnp.bfloat16),
            pltpu.VMEM(((HALF + 2) * SLOT, 2 * YC), jnp.bfloat16),
            pltpu.VMEM((ROWS, 3 * SLOT), jnp.bfloat16),
            pltpu.VMEM((ROWS, 3 * SLOT), jnp.bfloat16),
        ],
        compiler_params=params,
        name="decoder",
    )(
        patch_features.transpose(1, 2, 0, 3),
        conv1_weight.transpose(2, 3, 4, 0, 1),
        conv1_bias.reshape(1, CHANNELS),
        conv2_weight.transpose(2, 3, 4, 0, 1),
        conv2_bias.reshape(1, CHANNELS),
        head_weight.astype(f32).reshape(1, CHANNELS),
    )
    below = from_behind(patch, "gz", 1)
    above = from_behind(patch, "gz", -1)
    far_below = from_behind(high, "gz", 2)
    far_above = from_behind(low, "gz", -2)
    left, right = pl.pallas_call(
        slab_kernel,
        out_shape=(
            jax.ShapeDtypeStruct((216, YC), f32),
            jax.ShapeDtypeStruct((216, YC), f32),
        ),
        in_specs=whole(5),
        out_specs=tuple(whole(2)),
        compiler_params=params,
        name="slab",
    )(below, patch, above, far_below, far_above)
    from_left = from_behind(right, "xy", 1)
    from_right = from_behind(left, "xy", -1)
    place = jnp.stack(
        [
            lax.axis_index("gz"),
            jnp.int32(lax.axis_size("gz")),
            lax.axis_index("xy"),
            jnp.int32(lax.axis_size("xy")),
        ]
    ).astype(jnp.int32)
    x_upper, x_lower, y_all = filter_constants()
    probability, vesselness = pl.pallas_call(
        vessel_kernel,
        out_shape=(
            jax.ShapeDtypeStruct((CZ * CX, YC), f32),
            jax.ShapeDtypeStruct((CZ * CX, YC), f32),
        ),
        in_specs=[pl.BlockSpec(memory_space=pltpu.SMEM)] + whole(8),
        out_specs=tuple(whole(2)),
        scratch_shapes=[
            pltpu.VMEM((3 * CZ * 32, YC), f32),
            pltpu.VMEM((9 * 256, 2 * YC), jnp.bfloat16),
        ],
        compiler_params=params,
        name="vessel",
    )(
        place,
        left,
        right,
        from_left,
        from_right,
        tissue_mask.reshape(CZ * CX, YC),
        jnp.asarray(x_upper),
        jnp.asarray(x_lower),
        jnp.asarray(y_all),
    )
    return (
        probability.reshape(CZ, CX, YC),
        vesselness.reshape(CZ, CX, YC),
    )


def solution(mesh):
    placed = (P(None, "gz", "xy", None), P(), P(), P(), P(), P(), P("gz", "xy", None))
    return jax.shard_map(
        on_device,
        mesh=mesh,
        in_specs=placed,
        out_specs=(P("gz", "xy", None), P("gz", "xy", None)),
        check_vma=False,
    )
```

```python
import jax
import jax.numpy as jnp
import numpy as np
from jax import lax
from jax.experimental import pallas as pl
from jax.experimental.pallas import tpu as pltpu
from jax.sharding import PartitionSpec as P

CHANNELS = 16
CZ = 8
CX = 16
YC = 128
MARGIN = 1
RIM = 8
SPAN_Z = CZ + 2 * MARGIN
SPAN_X = CX + 2 * MARGIN
HALF = SPAN_X // 2
ROWS = SPAN_Z * CHANNELS
SLOT = 512
RADII = (RIM // 4, RIM // 2, RIM)
VESSEL_GAIN = 4.0
TUBE_FLOOR = 0.01
PATCH = SPAN_Z * CX + 2 * 16
CHIP_ROWS = 2 * CZ + 2
EDGE = 168
SEND_ROWS = CHIP_ROWS // 2
VMEM_LIMIT = 24 * 1024 * 1024
DECODER_VMEM_LIMIT = 63 * 1024 * 1024


def window(size):
    position = np.arange(size, dtype=np.float64)
    return np.exp(-0.5 * ((position - (size - 1) / 2.0) / (size / 4.0)) ** 2)


WINDOW_Z = window(SPAN_Z)
WINDOW_X = window(SPAN_X)


def taps(radius, degree):
    spread = radius / 3.0
    offsets = np.arange(-radius, radius + 1, dtype=np.float64)
    gaussian = np.exp(-offsets * offsets / (2.0 * spread * spread))
    gaussian = gaussian / gaussian.sum()
    if degree == 1:
        return -offsets / spread**2 * gaussian
    if degree == 2:
        return (offsets**2 / spread**4 - 1.0 / spread**2) * gaussian
    return gaussian


def band(out_len, in_len, offset, radius, degree):
    weights = taps(radius, degree)
    distance = np.arange(out_len)[:, None] + offset - np.arange(in_len)[None, :]
    inside = np.abs(distance) <= radius
    return np.where(inside, weights[np.clip(distance, -radius, radius) + radius], 0.0)


def split_terms(matrix):
    whole = matrix.astype(np.float32)
    upper = whole.astype(jnp.bfloat16)
    lower = (whole - upper.astype(np.float32)).astype(jnp.bfloat16)
    return upper, lower


def filter_constants():
    x_upper, x_lower, y_all = [], [], []
    for radius in RADII:
        blocks = [
            np.kron(np.eye(CZ), band(CX, CX + 2 * RIM, RIM, radius, degree)) for degree in range(3)
        ]
        upper, lower = split_terms(np.concatenate(blocks, axis=0))
        x_upper.append(upper)
        x_lower.append(lower)
        for degree in range(3):
            scaled = (radius / 3.0) ** 2 * band(YC, YC, 0, radius, degree).T
            upper, lower = split_terms(scaled)
            top = np.concatenate([upper, lower], axis=1)
            bottom = np.concatenate([upper, np.zeros_like(lower)], axis=1)
            y_all.append(np.concatenate([top, bottom], axis=0))
    return np.stack(x_upper), np.stack(x_lower), np.stack(y_all)


def iota(shape, dim):
    return lax.broadcasted_iota(jnp.int32, shape, dim)


def y_neighbours(values):
    lane = iota(values.shape, 1)
    before = jnp.where(lane == 0, 0.0, pltpu.roll(values, 1, 1))
    after = jnp.where(lane == YC - 1, 0.0, pltpu.roll(values, YC - 1, 1))
    return (before, values, after)


def store_column(slots_ref, slot, half, three):
    lanes = pl.ds(half * YC, YC)
    for dy in range(3):
        slots_ref[pl.ds(slot * SLOT + dy * ROWS, ROWS), lanes] = three[dy]


def expand_weight(weight_ref, wide_ref):
    lane = iota((CHANNELS, SLOT), 1)
    group = (lane >= ROWS).astype(jnp.int32) + (lane >= 2 * ROWS).astype(jnp.int32) + (
        lane >= 3 * ROWS
    ).astype(jnp.int32)
    row = iota((CHANNELS, SLOT), 0)
    same = (lane & (CHANNELS - 1)) == row
    spread = jnp.zeros((9 * CHANNELS, SLOT), jnp.float32)
    for dy in range(3):
        pick = jnp.where(same & (group == dy), 1.0, 0.0).astype(jnp.bfloat16)
        part = weight_ref[:, :, dy].reshape(9 * CHANNELS, CHANNELS)
        spread = spread + jnp.dot(part, pick, preferred_element_type=jnp.float32)
    plane = (lane - group * ROWS) >> 4
    for dx in range(3):
        three = [
            spread[(dz * 3 + dx) * CHANNELS : (dz * 3 + dx + 1) * CHANNELS] for dz in range(3)
        ]
        for z in range(SPAN_Z):
            rows = jnp.where(
                plane == z - 1,
                three[0],
                jnp.where(plane == z, three[1], jnp.where(plane == z + 1, three[2], 0.0)),
            )
            wide_ref[z * CHANNELS : (z + 1) * CHANNELS, dx * SLOT : (dx + 1) * SLOT] = rows.astype(
                jnp.bfloat16
            )


def column_of(row_ref):
    eye = iota((CHANNELS, CHANNELS), 0) == iota((CHANNELS, CHANNELS), 1)
    row = row_ref[...].astype(jnp.float32)
    return jnp.sum(jnp.where(eye, row, 0.0), axis=1, keepdims=True)


def decoder_kernel(
    features_hbm,
    weight1_hbm,
    bias1_hbm,
    weight2_hbm,
    bias2_hbm,
    head_hbm,
    patch_ref,
    features_ref,
    weight1_ref,
    bias1_ref,
    weight2_ref,
    bias2_ref,
    head_ref,
    first_ref,
    second_ref,
    wide1_ref,
    wide2_ref,
    arrived,
):
    routes = (
        (weight1_hbm, weight1_ref),
        (weight2_hbm, weight2_ref),
        (bias1_hbm, bias1_ref),
        (bias2_hbm, bias2_ref),
        (head_hbm, head_ref),
        (features_hbm, features_ref),
    )
    copies = [
        pltpu.make_async_copy(source, target, arrived.at[k])
        for k, (source, target) in enumerate(routes)
    ]
    for copy in copies:
        copy.start()
    for ref in (first_ref, second_ref):
        ref[0:SLOT, 0:YC] = jnp.zeros((SLOT, YC), jnp.bfloat16)
        ref[(HALF + 1) * SLOT :, YC:] = jnp.zeros((SLOT, YC), jnp.bfloat16)
        for slot in range(HALF + 2):
            ref[slot * SLOT + 3 * ROWS : (slot + 1) * SLOT, :] = jnp.zeros(
                (SLOT - 3 * ROWS, 2 * YC), jnp.bfloat16
            )
    copies[0].wait()
    expand_weight(weight1_ref, wide1_ref)
    copies[1].wait()
    expand_weight(weight2_ref, wide2_ref)
    for copy in copies[2:]:
        copy.wait()
    for x in range(SPAN_X):
        column = features_ref[:, x].reshape(ROWS, YC).astype(jnp.float32)
        three = [v.astype(jnp.bfloat16) for v in y_neighbours(column)]
        if x <= HALF:
            store_column(first_ref, x + 1, 0, three)
        if x >= HALF - 1:
            store_column(first_ref, x - HALF + 1, 1, three)

    def layer(wide_ref, slots_ref, bias, step):
        summed = jnp.dot(
            wide_ref[...],
            slots_ref[step * SLOT : (step + 3) * SLOT, :],
            preferred_element_type=jnp.float32,
        )
        shaped = summed.reshape(SPAN_Z, CHANNELS, 2 * YC) + bias[None]
        return jnp.maximum(shaped, 0.0).reshape(ROWS, 2 * YC)

    bias1 = column_of(bias1_ref)
    for step in range(HALF):
        hidden = layer(wide1_ref, first_ref, bias1, step)
        for half in range(2):
            part = hidden[:, half * YC : (half + 1) * YC]
            three = [v.astype(jnp.bfloat16) for v in y_neighbours(part)]
            store_column(second_ref, step + 1, half, three)
            if half == 0 and step == HALF - 1:
                store_column(second_ref, 0, 1, three)
            if half == 1 and step == 0:
                store_column(second_ref, HALF + 1, 0, three)

    bias2 = column_of(bias2_ref)
    repeat = ((iota((CHANNELS, ROWS), 1) & (CHANNELS - 1)) == iota((CHANNELS, ROWS), 0)).astype(
        jnp.float32
    )
    head_lanes = jnp.sum(
        repeat * column_of(head_ref), axis=0, keepdims=True
    )
    head = jnp.where(
        (iota((16, ROWS), 1) >> 4) == iota((16, ROWS), 0), head_lanes, 0.0
    ).astype(jnp.bfloat16)
    place = iota((16, YC), 0).astype(jnp.float32)
    centred = (place - (SPAN_Z - 1) / 2.0) / (SPAN_Z / 4.0)
    weight_z = jnp.exp(-0.5 * centred * centred)
    for step in range(HALF):
        hidden = layer(wide2_ref, second_ref, bias2, step).astype(jnp.bfloat16)
        logits = jnp.dot(head, hidden, preferred_element_type=jnp.float32)
        for half in range(2):
            x = step + half * HALF
            weighted = logits[:, half * YC : (half + 1) * YC] * (weight_z * float(WINDOW_X[x]))
            if x == 0 or x == SPAN_X - 1:
                side = 0 if x == 0 else 1
                patch_ref[160 + side * 16 : 176 + side * 16, :] = weighted
            else:
                patch_ref[pl.ds(x - 1, SPAN_Z, stride=CX), :] = weighted[:SPAN_Z]


def chip_row(pair_ref, r):
    low, high = r + 1, r - CZ + 1
    value = None
    for patch, index in ((0, low), (1, high)):
        if 0 <= index < SPAN_Z:
            base = patch * PATCH + index * CX
            part = pair_ref[base : base + CX, :]
            value = part if value is None else value + part
    return value


def chip_margin(pair_ref, side, r):
    low, high = r + 1, r - CZ + 1
    value = None
    for patch, index in ((0, low), (1, high)):
        if 0 <= index < SPAN_Z:
            base = patch * PATCH + SPAN_Z * CX + side * 16 + index
            part = pair_ref[base : base + 1, :]
            value = part if value is None else value + part
    return value


def edge_kernel(place_ref, pair_ref, edge_ref):
    to_right = place_ref[4] == 1
    for n in range(CHIP_ROWS):
        value = chip_row(pair_ref, n - 1)
        edge_ref[n * 8 : (n + 1) * 8, :] = jnp.where(to_right, value[8:], value[:8])
        left, right = (chip_margin(pair_ref, side, n - 1) for side in range(2))
        edge_ref[CHIP_ROWS * 8 + n : CHIP_ROWS * 8 + n + 1, :] = jnp.where(to_right, right, left)
    edge_ref[CHIP_ROWS * 9 :, :] = jnp.zeros((EDGE - CHIP_ROWS * 9, YC), jnp.float32)


def chip_kernel(place_ref, pair_ref, edges_ref, chip_ref, send_ref):
    at_x, count_x, odd_x = place_ref[2], place_ref[3], place_ref[5]
    from_left = (1 - odd_x) * (2 * EDGE)
    from_right = odd_x * (2 * EDGE) + EDGE
    sub = iota((8, YC), 0)
    has_left = jnp.where(at_x > 0, 1.0, 0.0)
    has_right = jnp.where(at_x < count_x - 1, 1.0, 0.0)
    upper_core = place_ref[6] == 1

    def part(start, offset, count):
        return edges_ref[pl.ds(pl.multiple_of(start, 8) + offset, count), :]

    left_margins = [part(from_left, CHIP_ROWS * 8 + 8 * n, 8) * has_left for n in range(3)]
    right_margins = [part(from_right, CHIP_ROWS * 8 + 8 * n, 8) * has_right for n in range(3)]
    for n in range(CHIP_ROWS):
        own = chip_row(pair_ref, n - 1)
        first_margin, last_margin = (chip_margin(pair_ref, side, n - 1) for side in range(2))
        block, at = divmod(n, 8)
        left_margin = left_margins[block][at : at + 1]
        right_margin = right_margins[block][at : at + 1]
        sums = (
            part(from_left, n * 8, 8) * has_left + jnp.where(sub == 7, first_margin, 0.0),
            own[:8] + jnp.where(sub == 0, left_margin, 0.0),
            own[8:] + jnp.where(sub == 7, right_margin, 0.0),
            part(from_right, n * 8, 8) * has_right + jnp.where(sub == 0, last_margin, 0.0),
        )
        for k in range(4):
            at = n * 32 + k * 8
            chip_ref[at : at + 8, :] = sums[k]
            low = k * 8 + n * 32
            high = k * 8 + (n - SEND_ROWS) * 32
            if n < SEND_ROWS:

                @pl.when(jnp.logical_not(upper_core))
                def _(value=sums[k], low=low):
                    send_ref[low : low + 8, :] = value

            else:

                @pl.when(upper_core)
                def _(value=sums[k], high=high):
                    send_ref[high : high + 8, :] = value


def two_terms(values):
    upper = values.astype(jnp.bfloat16)
    lower = (values - upper.astype(jnp.float32)).astype(jnp.bfloat16)
    return upper, lower


def vessel_kernel(
    place_ref,
    chip_ref,
    slabs_ref,
    rows_ref,
    tissue_ref,
    x_upper_ref,
    x_lower_ref,
    y_ref,
    probability_ref,
    vessel_ref,
    extended_ref,
    along_z_ref,
):
    upper_core = place_ref[6] == 1

    below = jnp.where(place_ref[0] - place_ref[6] > 0, 1.0, 0.0)
    above = jnp.where(place_ref[0] - place_ref[6] < place_ref[1] - 2, 1.0, 0.0)

    @pl.when(jnp.logical_not(upper_core))
    def _():
        for z in range(3 * CZ):
            value = None
            if z >= RIM - 1:
                n = z - RIM + 1
                value = chip_ref[n * 32 : (n + 1) * 32, :]
            if z < SEND_ROWS:
                part = slabs_ref[z * 32 : (z + 1) * 32, :] * below
                value = part if value is None else value + part
            if z == 3 * CZ - 1:
                value = value + rows_ref[32:64, :] * above
            extended_ref[z * 32 : (z + 1) * 32, :] = value

    @pl.when(upper_core)
    def _():
        for z in range(3 * CZ):
            value = None
            if z + 1 < CHIP_ROWS:
                value = chip_ref[(z + 1) * 32 : (z + 2) * 32, :]
            if z >= 3 * CZ - SEND_ROWS:
                n = SEND_ROWS + z - (3 * CZ - SEND_ROWS)
                part = slabs_ref[n * 32 : (n + 1) * 32, :] * above
                value = part if value is None else value + part
            if z == 0:
                value = value + rows_ref[0:32, :] * below
            extended_ref[z * 32 : (z + 1) * 32, :] = value

    at_z, count_z, at_x, count_x = (place_ref[k] for k in range(4))
    sub = iota((8, YC), 0)

    def inverse_x(first, edge, edge_row, present):
        cover = jnp.zeros((8, YC), jnp.float32)
        for j in range(8):
            cover = jnp.where(sub == j, float(WINDOW_X[first + j + 1]), cover)
        extra = jnp.where(present, float(edge), 0.0)
        return 1.0 / (cover + jnp.where(sub == edge_row, extra, 0.0))

    wx_last, wx_first = WINDOW_X[SPAN_X - 1], WINDOW_X[0]
    yes = at_x >= 0
    inverse = [
        inverse_x(8, wx_first, 7, yes),
        inverse_x(0, wx_last, 0, at_x > 0),
        inverse_x(8, wx_first, 7, at_x < count_x - 1),
        inverse_x(0, wx_last, 0, yes),
    ]
    wz_last, wz_first = WINDOW_Z[SPAN_Z - 1], WINDOW_Z[0]
    lower_there = (at_z > 1, at_z > 0, yes)
    upper_there = (yes, at_z < count_z - 1, at_z < count_z - 2)
    inside_x = (at_x > 0, yes, yes, at_x < count_x - 1)
    inside_z = (at_z > 0, yes, at_z < count_z - 1)
    keep_x = [jnp.where(flag, 1.0, 0.0) for flag in inside_x]
    keep_z = [jnp.where(flag, 1.0, 0.0) for flag in inside_z]
    for z in range(3 * CZ):
        block, i = divmod(z, CZ)
        plain = WINDOW_Z[i + 1]
        scale = float(1.0 / plain)
        if i == 0:
            scale = jnp.where(lower_there[block], float(1.0 / (plain + wz_last)), scale)
        if i == CZ - 1:
            scale = jnp.where(upper_there[block], float(1.0 / (plain + wz_first)), scale)
        for k in range(4):
            blended = extended_ref[z * 32 + k * 8 : z * 32 + k * 8 + 8, :]
            value = 1.0 / (1.0 + jnp.exp(-(blended * (inverse[k] * scale))))
            if block == 1 and k in (1, 2):
                at = i * CX + (k - 1) * 8
                probability_ref[at : at + 8, :] = value
            else:
                value = value * (keep_x[k] * keep_z[block])
            extended_ref[z * 32 + k * 8 : z * 32 + k * 8 + 8, :] = value

    weights = [[taps(radius, degree) for degree in range(3)] for radius in RADII]

    def one_plane(i, carry):
        def plane(offset):
            return extended_ref[pl.ds(pl.multiple_of((i + RIM + offset) * 32, 32), 32), :]

        centre = plane(0)
        results = {}
        for n, radius in enumerate(RADII):
            for degree in (0, 2):
                results[n, degree] = centre * float(weights[n][degree][radius])
        for k in range(1, RIM + 1):
            before, after = plane(-k), plane(k)
            both, change = before + after, before - after
            for n, radius in enumerate(RADII):
                if k > radius:
                    continue
                for degree in range(3):
                    term = (change if degree == 1 else both) * float(weights[n][degree][radius + k])
                    if (n, degree) in results:
                        results[n, degree] = results[n, degree] + term
                    else:
                        results[n, degree] = term
        for n in range(3):
            for degree in range(3):
                upper, lower = two_terms(results[n, degree])
                rows = pl.ds(pl.multiple_of((n * 3 + degree) * 256 + i * 32, 32), 32)
                along_z_ref[rows, 0:YC] = upper
                along_z_ref[rows, YC : 2 * YC] = lower
        return carry

    lax.fori_loop(0, CZ, one_plane, 0)

    total = jnp.zeros((CZ * CX, YC), jnp.float32)
    for n in range(3):
        after_x = {}
        for degree in range(3):
            count = (3 - degree) * 128
            data = along_z_ref[(n * 3 + degree) * 256 : (n * 3 + degree + 1) * 256, :]
            wide = jnp.dot(x_upper_ref[n, :count], data, preferred_element_type=jnp.float32)
            narrow = jnp.dot(
                x_lower_ref[n, :count], data[:, :YC], preferred_element_type=jnp.float32
            )
            summed = wide[:, :YC] + wide[:, YC:] + narrow
            for other in range(3 - degree):
                after_x[degree, other] = summed[other * 128 : (other + 1) * 128]

        def along_y(degree, keys):
            stacked = jnp.concatenate([after_x[key] for key in keys], axis=0)
            pair = jnp.concatenate(two_terms(stacked), axis=1)
            wide = jnp.dot(pair, y_ref[n * 3 + degree], preferred_element_type=jnp.float32)
            summed = wide[:, :YC] + wide[:, YC:]
            return [summed[at * 128 : (at + 1) * 128] for at in range(len(keys))]

        hzz, hxx, hzx = along_y(0, ((2, 0), (0, 2), (1, 1)))
        hzy, hxy = along_y(1, ((1, 0), (0, 1)))
        (hyy,) = along_y(2, ((0, 0),))
        first_inv = hzz + hxx + hyy
        second_inv = hzz * hxx + hzz * hyy + hxx * hyy - hzx * hzx - hzy * hzy - hxy * hxy
        third_inv = (
            hzz * (hxx * hyy - hxy * hxy)
            - hzx * (hzx * hyy - hxy * hzy)
            + hzy * (hzx * hxy - hxx * hzy)
        )
        positive = jnp.maximum(second_inv, 0.0)
        size = jnp.abs(third_inv)
        root = jnp.where(size > 0.0, jnp.exp(jnp.log(size) * (2.0 / 3.0)), 0.0)
        total = total + jnp.maximum(-first_inv, 0.0) * positive / (positive + root + TUBE_FLOOR)
    vessel_ref[...] = VESSEL_GAIN * tissue_ref[...].astype(jnp.float32) * total


def pairs_of(kind, count_z, count_x):
    def flat(z, x):
        return (z % count_z) * count_x + x % count_x

    if kind == "x":
        return [
            [flat(z, x), flat(z, x + 1)]
            for z in range(count_z)
            for x in range(z % 2, count_x + z % 2, 2)
        ]
    first = 0 if kind == "chip" else 1
    return [
        [flat(z, x), flat(z + 1, x)]
        for z in range(first, count_z + first, 2)
        for x in range(count_x)
    ]


def swap(block, kind):
    groups = pairs_of(kind, lax.axis_size("gz"), lax.axis_size("xy"))
    return lax.all_gather(block, ("gz", "xy"), axis_index_groups=groups, tiled=True)


def whole(count, space=pltpu.VMEM):
    return [pl.BlockSpec(memory_space=space)] * count


def shape_of(*dims):
    return jax.ShapeDtypeStruct(dims, jnp.float32)


def on_device(
    patch_features, conv1_weight, conv1_bias, conv2_weight, conv2_bias, head_weight, tissue_mask
):
    f32, bf16 = jnp.float32, jnp.bfloat16
    params = pltpu.CompilerParams(vmem_limit_bytes=VMEM_LIMIT)
    at_z, at_x = lax.axis_index("gz"), lax.axis_index("xy")
    place = jnp.stack(
        [
            at_z,
            jnp.int32(lax.axis_size("gz")),
            at_x,
            jnp.int32(lax.axis_size("xy")),
            1 - ((at_z + at_x) & 1),
            at_x & 1,
            at_z & 1,
        ]
    ).astype(jnp.int32)
    weight_shape = (3, 3, 3, CHANNELS, CHANNELS)
    slots = ((HALF + 2) * SLOT, 2 * YC)
    patch = pl.pallas_call(
        decoder_kernel,
        out_shape=shape_of(PATCH, YC),
        in_specs=whole(6, pltpu.HBM),
        out_specs=whole(1)[0],
        scratch_shapes=[
            pltpu.VMEM((SPAN_Z, SPAN_X, CHANNELS, YC), bf16),
            pltpu.VMEM(weight_shape, bf16),
            pltpu.VMEM((1, CHANNELS), f32),
            pltpu.VMEM(weight_shape, bf16),
            pltpu.VMEM((1, CHANNELS), f32),
            pltpu.VMEM((1, CHANNELS), bf16),
            pltpu.VMEM(slots, bf16),
            pltpu.VMEM(slots, bf16),
            pltpu.VMEM((ROWS, 3 * SLOT), bf16),
            pltpu.VMEM((ROWS, 3 * SLOT), bf16),
            pltpu.SemaphoreType.DMA((6,)),
        ],
        compiler_params=pltpu.CompilerParams(vmem_limit_bytes=DECODER_VMEM_LIMIT),
        name="decoder",
    )(
        patch_features.transpose(1, 2, 0, 3),
        conv1_weight.transpose(2, 3, 4, 0, 1),
        conv1_bias.reshape(1, CHANNELS),
        conv2_weight.transpose(2, 3, 4, 0, 1),
        conv2_bias.reshape(1, CHANNELS),
        head_weight.reshape(1, CHANNELS),
    )
    smem = pl.BlockSpec(memory_space=pltpu.SMEM)
    pair = swap(patch, "chip")
    edge = pl.pallas_call(
        edge_kernel,
        out_shape=shape_of(EDGE, YC),
        in_specs=[smem] + whole(1),
        out_specs=whole(1)[0],
        compiler_params=params,
        name="edge",
    )(place, pair)
    edges = swap(swap(edge, "x"), "chip")
    chip, send = pl.pallas_call(
        chip_kernel,
        out_shape=(shape_of(CHIP_ROWS * 32, YC), shape_of(SEND_ROWS * 32, YC)),
        in_specs=[smem] + whole(2),
        out_specs=tuple(whole(2)),
        compiler_params=params,
        name="chip",
    )(place, pair, edges)
    slabs = swap(send, "slab")
    upper_core = at_z & 1
    row_at = jnp.where(upper_core == 1, SEND_ROWS * 32, (SEND_ROWS - 1) * 32)
    rows = swap(lax.dynamic_slice(slabs, (row_at, 0), (32, YC)), "chip")
    x_upper, x_lower, y_all = filter_constants()
    probability, vesselness = pl.pallas_call(
        vessel_kernel,
        out_shape=(shape_of(CZ * CX, YC), shape_of(CZ * CX, YC)),
        in_specs=[smem] + whole(7),
        out_specs=tuple(whole(2)),
        scratch_shapes=[
            pltpu.VMEM((3 * CZ * 32, YC), f32),
            pltpu.VMEM((9 * 256, 2 * YC), bf16),
        ],
        compiler_params=params,
        name="vessel",
    )(
        place,
        chip,
        slabs,
        rows,
        tissue_mask.reshape(CZ * CX, YC),
        jnp.asarray(x_upper),
        jnp.asarray(x_lower),
        jnp.asarray(y_all),
    )
    return (
        probability.reshape(CZ, CX, YC),
        vesselness.reshape(CZ, CX, YC),
    )


def solution(mesh):
    placed = (P(None, "gz", "xy", None), P(), P(), P(), P(), P(), P("gz", "xy", None))
    return jax.shard_map(
        on_device,
        mesh=mesh,
        in_specs=placed,
        out_specs=(P("gz", "xy", None), P("gz", "xy", None)),
        check_vma=False,
    )
```

```python
import jax
import jax.numpy as jnp
import numpy as np
from jax import lax
from jax.experimental import pallas as pl
from jax.experimental.pallas import tpu as pltpu
from jax.sharding import PartitionSpec as P

CHANNELS = 16
CZ = 8
CX = 16
YC = 128
MARGIN = 1
RIM = 8
SPAN_Z = CZ + 2 * MARGIN
SPAN_X = CX + 2 * MARGIN
HALF = SPAN_X // 2
ROWS = SPAN_Z * CHANNELS
SLOT = 512
RADII = (RIM // 4, RIM // 2, RIM)
VESSEL_GAIN = 4.0
TUBE_FLOOR = 0.01
PATCH = SPAN_Z * CX + 2 * 16
CHIP_ROWS = 2 * CZ + 2
EDGE = 168
SEND_ROWS = CHIP_ROWS // 2
VMEM_LIMIT = 24 * 1024 * 1024
DECODER_VMEM_LIMIT = 63 * 1024 * 1024


def window(size):
    position = np.arange(size, dtype=np.float64)
    return np.exp(-0.5 * ((position - (size - 1) / 2.0) / (size / 4.0)) ** 2)


WINDOW_Z = window(SPAN_Z)
WINDOW_X = window(SPAN_X)


def taps(radius, degree):
    spread = radius / 3.0
    offsets = np.arange(-radius, radius + 1, dtype=np.float64)
    gaussian = np.exp(-offsets * offsets / (2.0 * spread * spread))
    gaussian = gaussian / gaussian.sum()
    if degree == 1:
        return -offsets / spread**2 * gaussian
    if degree == 2:
        return (offsets**2 / spread**4 - 1.0 / spread**2) * gaussian
    return gaussian


def band(out_len, in_len, offset, radius, degree):
    weights = taps(radius, degree)
    distance = np.arange(out_len)[:, None] + offset - np.arange(in_len)[None, :]
    inside = np.abs(distance) <= radius
    return np.where(inside, weights[np.clip(distance, -radius, radius) + radius], 0.0)


def split_terms(matrix):
    whole = matrix.astype(np.float32)
    upper = whole.astype(jnp.bfloat16)
    lower = (whole - upper.astype(np.float32)).astype(jnp.bfloat16)
    return upper, lower


def filter_constants():
    x_upper, x_lower, y_all = [], [], []
    for radius in RADII:
        blocks = [
            np.kron(np.eye(CZ), band(CX, CX + 2 * RIM, RIM, radius, degree)) for degree in range(3)
        ]
        upper, lower = split_terms(np.concatenate(blocks, axis=0))
        x_upper.append(upper)
        x_lower.append(lower)
        for degree in range(3):
            scaled = (radius / 3.0) ** 2 * band(YC, YC, 0, radius, degree).T
            upper, lower = split_terms(scaled)
            top = np.concatenate([upper, lower], axis=1)
            bottom = np.concatenate([upper, np.zeros_like(lower)], axis=1)
            y_all.append(np.concatenate([top, bottom], axis=0))
    return np.stack(x_upper), np.stack(x_lower), np.stack(y_all)


def iota(shape, dim):
    return lax.broadcasted_iota(jnp.int32, shape, dim)


def y_neighbours(values):
    lane = iota(values.shape, 1)
    before = jnp.where(lane == 0, 0.0, pltpu.roll(values, 1, 1))
    after = jnp.where(lane == YC - 1, 0.0, pltpu.roll(values, YC - 1, 1))
    return (before, values, after)


def store_column(slots_ref, slot, half, three):
    lanes = pl.ds(half * YC, YC)
    for dy in range(3):
        slots_ref[pl.ds(slot * SLOT + dy * ROWS, ROWS), lanes] = three[dy]


def expand_weight(weight_ref, wide_ref):
    lane = iota((CHANNELS, SLOT), 1)
    group = (lane >= ROWS).astype(jnp.int32) + (lane >= 2 * ROWS).astype(jnp.int32) + (
        lane >= 3 * ROWS
    ).astype(jnp.int32)
    row = iota((CHANNELS, SLOT), 0)
    same = (lane & (CHANNELS - 1)) == row
    spread = jnp.zeros((9 * CHANNELS, SLOT), jnp.float32)
    for dy in range(3):
        pick = jnp.where(same & (group == dy), 1.0, 0.0).astype(jnp.bfloat16)
        part = weight_ref[:, :, dy].reshape(9 * CHANNELS, CHANNELS)
        spread = spread + jnp.dot(part, pick, preferred_element_type=jnp.float32)
    plane = (lane - group * ROWS) >> 4
    for dx in range(3):
        three = [
            spread[(dz * 3 + dx) * CHANNELS : (dz * 3 + dx + 1) * CHANNELS] for dz in range(3)
        ]
        for z in range(SPAN_Z):
            rows = jnp.where(
                plane == z - 1,
                three[0],
                jnp.where(plane == z, three[1], jnp.where(plane == z + 1, three[2], 0.0)),
            )
            wide_ref[z * CHANNELS : (z + 1) * CHANNELS, dx * SLOT : (dx + 1) * SLOT] = rows.astype(
                jnp.bfloat16
            )


def column_of(row_ref):
    eye = iota((CHANNELS, CHANNELS), 0) == iota((CHANNELS, CHANNELS), 1)
    row = row_ref[...].astype(jnp.float32)
    return jnp.sum(jnp.where(eye, row, 0.0), axis=1, keepdims=True)


def decoder_kernel(
    features_hbm,
    weight1_hbm,
    bias1_hbm,
    weight2_hbm,
    bias2_hbm,
    head_hbm,
    patch_ref,
    features_ref,
    weight1_ref,
    bias1_ref,
    weight2_ref,
    bias2_ref,
    head_ref,
    first_ref,
    second_ref,
    wide1_ref,
    wide2_ref,
    last_ref,
    arrived,
):
    routes = (
        (weight1_hbm, weight1_ref),
        (weight2_hbm, weight2_ref),
        (bias1_hbm, bias1_ref),
        (bias2_hbm, bias2_ref),
        (head_hbm, head_ref),
        (features_hbm, features_ref),
    )
    copies = [
        pltpu.make_async_copy(source, target, arrived.at[k])
        for k, (source, target) in enumerate(routes)
    ]
    for copy in copies:
        copy.start()
    for ref in (first_ref, second_ref):
        ref[0:SLOT, 0:YC] = jnp.zeros((SLOT, YC), jnp.bfloat16)
        ref[(HALF + 1) * SLOT :, YC:] = jnp.zeros((SLOT, YC), jnp.bfloat16)
        for slot in range(HALF + 2):
            ref[slot * SLOT + 3 * ROWS : (slot + 1) * SLOT, :] = jnp.zeros(
                (SLOT - 3 * ROWS, 2 * YC), jnp.bfloat16
            )
    copies[0].wait()
    expand_weight(weight1_ref, wide1_ref)
    copies[1].wait()
    expand_weight(weight2_ref, wide2_ref)
    for copy in copies[2:]:
        copy.wait()
    for x in range(SPAN_X):
        column = features_ref[:, x].reshape(ROWS, YC).astype(jnp.float32)
        three = [v.astype(jnp.bfloat16) for v in y_neighbours(column)]
        if x <= HALF:
            store_column(first_ref, x + 1, 0, three)
        if x >= HALF - 1:
            store_column(first_ref, x - HALF + 1, 1, three)

    def layer(wide_ref, slots_ref, bias, step):
        summed = jnp.dot(
            wide_ref[...],
            slots_ref[step * SLOT : (step + 3) * SLOT, :],
            preferred_element_type=jnp.float32,
        )
        shaped = summed.reshape(SPAN_Z, CHANNELS, 2 * YC) + bias[None]
        return jnp.maximum(shaped, 0.0).reshape(ROWS, 2 * YC)

    bias1 = column_of(bias1_ref)
    for step in range(HALF):
        hidden = layer(wide1_ref, first_ref, bias1, step)
        for half in range(2):
            part = hidden[:, half * YC : (half + 1) * YC]
            three = [v.astype(jnp.bfloat16) for v in y_neighbours(part)]
            store_column(second_ref, step + 1, half, three)
            if half == 0 and step == HALF - 1:
                store_column(second_ref, 0, 1, three)
            if half == 1 and step == 0:
                store_column(second_ref, HALF + 1, 0, three)

    bias2 = column_of(bias2_ref)
    repeat = ((iota((CHANNELS, ROWS), 1) & (CHANNELS - 1)) == iota((CHANNELS, ROWS), 0)).astype(
        jnp.float32
    )
    head_lanes = jnp.sum(
        repeat * column_of(head_ref), axis=0, keepdims=True
    )
    head = jnp.where(
        (iota((16, ROWS), 1) >> 4) == iota((16, ROWS), 0), head_lanes, 0.0
    ).astype(jnp.bfloat16)
    place = iota((16, YC), 0).astype(jnp.float32)
    centred = (place - (SPAN_Z - 1) / 2.0) / (SPAN_Z / 4.0)
    weight_z = jnp.exp(-0.5 * centred * centred)
    for step in range(HALF):
        hidden = layer(wide2_ref, second_ref, bias2, step).astype(jnp.bfloat16)
        last_ref[:, step * 2 * YC : (step + 1) * 2 * YC] = hidden
    logits = jnp.dot(head, last_ref[...], preferred_element_type=jnp.float32)
    for step in range(HALF):
        for half in range(2):
            x = step + half * HALF
            at = (step * 2 + half) * YC
            weighted = logits[:, at : at + YC] * (weight_z * float(WINDOW_X[x]))
            if x == 0 or x == SPAN_X - 1:
                side = 0 if x == 0 else 1
                patch_ref[160 + side * 16 : 176 + side * 16, :] = weighted
            else:
                patch_ref[pl.ds(x - 1, SPAN_Z, stride=CX), :] = weighted[:SPAN_Z]


def chip_row(pair_ref, r):
    low, high = r + 1, r - CZ + 1
    value = None
    for patch, index in ((0, low), (1, high)):
        if 0 <= index < SPAN_Z:
            base = patch * PATCH + index * CX
            part = pair_ref[base : base + CX, :]
            value = part if value is None else value + part
    return value


def chip_margin(pair_ref, side, r):
    low, high = r + 1, r - CZ + 1
    value = None
    for patch, index in ((0, low), (1, high)):
        if 0 <= index < SPAN_Z:
            base = patch * PATCH + SPAN_Z * CX + side * 16 + index
            part = pair_ref[base : base + 1, :]
            value = part if value is None else value + part
    return value


def position():
    return lax.axis_index("gz"), lax.axis_size("gz"), lax.axis_index("xy"), lax.axis_size("xy")


def edge_kernel(pair_ref, edge_ref):
    at_z, _, at_x, _ = position()
    to_right = ((at_z + at_x) & 1) == 0
    for n in range(CHIP_ROWS):
        value = chip_row(pair_ref, n - 1)
        edge_ref[n * 8 : (n + 1) * 8, :] = jnp.where(to_right, value[8:], value[:8])
        left, right = (chip_margin(pair_ref, side, n - 1) for side in range(2))
        edge_ref[CHIP_ROWS * 8 + n : CHIP_ROWS * 8 + n + 1, :] = jnp.where(to_right, right, left)
    edge_ref[CHIP_ROWS * 9 :, :] = jnp.zeros((EDGE - CHIP_ROWS * 9, YC), jnp.float32)


def chip_kernel(pair_ref, edges_ref, chip_ref, send_ref):
    at_z, _, at_x, count_x = position()
    odd_x = at_x & 1
    from_left = (1 - odd_x) * (2 * EDGE)
    from_right = odd_x * (2 * EDGE) + EDGE
    sub = iota((8, YC), 0)
    has_left = jnp.where(at_x > 0, 1.0, 0.0)
    has_right = jnp.where(at_x < count_x - 1, 1.0, 0.0)
    upper_core = (at_z & 1) == 1

    def part(start, offset, count):
        return edges_ref[pl.ds(pl.multiple_of(start, 8) + offset, count), :]

    left_margins = [part(from_left, CHIP_ROWS * 8 + 8 * n, 8) * has_left for n in range(3)]
    right_margins = [part(from_right, CHIP_ROWS * 8 + 8 * n, 8) * has_right for n in range(3)]
    for n in range(CHIP_ROWS):
        own = chip_row(pair_ref, n - 1)
        first_margin, last_margin = (chip_margin(pair_ref, side, n - 1) for side in range(2))
        block, at = divmod(n, 8)
        left_margin = left_margins[block][at : at + 1]
        right_margin = right_margins[block][at : at + 1]
        sums = (
            part(from_left, n * 8, 8) * has_left + jnp.where(sub == 7, first_margin, 0.0),
            own[:8] + jnp.where(sub == 0, left_margin, 0.0),
            own[8:] + jnp.where(sub == 7, right_margin, 0.0),
            part(from_right, n * 8, 8) * has_right + jnp.where(sub == 0, last_margin, 0.0),
        )
        for k in range(4):
            at = n * 32 + k * 8
            chip_ref[at : at + 8, :] = sums[k]
            low = k * 8 + n * 32
            high = k * 8 + (n - SEND_ROWS) * 32
            if n < SEND_ROWS:

                @pl.when(jnp.logical_not(upper_core))
                def _(value=sums[k], low=low):
                    send_ref[low : low + 8, :] = value

            else:

                @pl.when(upper_core)
                def _(value=sums[k], high=high):
                    send_ref[high : high + 8, :] = value


def two_terms(values):
    upper = values.astype(jnp.bfloat16)
    lower = (values - upper.astype(jnp.float32)).astype(jnp.bfloat16)
    return upper, lower


def vessel_kernel(
    chip_ref,
    slabs_ref,
    rows_ref,
    tissue_ref,
    x_upper_ref,
    x_lower_ref,
    y_ref,
    probability_ref,
    vessel_ref,
    extended_ref,
    along_z_ref,
):
    at_z, count_z, at_x, count_x = position()
    upper_core = (at_z & 1) == 1
    below = jnp.where(at_z - (at_z & 1) > 0, 1.0, 0.0)
    above = jnp.where(at_z - (at_z & 1) < count_z - 2, 1.0, 0.0)

    @pl.when(jnp.logical_not(upper_core))
    def _():
        for z in range(3 * CZ):
            value = None
            if z >= RIM - 1:
                n = z - RIM + 1
                value = chip_ref[n * 32 : (n + 1) * 32, :]
            if z < SEND_ROWS:
                part = slabs_ref[z * 32 : (z + 1) * 32, :] * below
                value = part if value is None else value + part
            if z == 3 * CZ - 1:
                value = value + rows_ref[32:64, :] * above
            extended_ref[z * 32 : (z + 1) * 32, :] = value

    @pl.when(upper_core)
    def _():
        for z in range(3 * CZ):
            value = None
            if z + 1 < CHIP_ROWS:
                value = chip_ref[(z + 1) * 32 : (z + 2) * 32, :]
            if z >= 3 * CZ - SEND_ROWS:
                n = SEND_ROWS + z - (3 * CZ - SEND_ROWS)
                part = slabs_ref[n * 32 : (n + 1) * 32, :] * above
                value = part if value is None else value + part
            if z == 0:
                value = value + rows_ref[0:32, :] * below
            extended_ref[z * 32 : (z + 1) * 32, :] = value

    sub = iota((8, YC), 0)

    def inverse_x(first, edge, edge_row, present):
        cover = jnp.zeros((8, YC), jnp.float32)
        for j in range(8):
            cover = jnp.where(sub == j, float(WINDOW_X[first + j + 1]), cover)
        extra = jnp.where(present, float(edge), 0.0)
        return 1.0 / (cover + jnp.where(sub == edge_row, extra, 0.0))

    wx_last, wx_first = WINDOW_X[SPAN_X - 1], WINDOW_X[0]
    yes = at_x >= 0
    inverse = [
        inverse_x(8, wx_first, 7, yes),
        inverse_x(0, wx_last, 0, at_x > 0),
        inverse_x(8, wx_first, 7, at_x < count_x - 1),
        inverse_x(0, wx_last, 0, yes),
    ]
    wz_last, wz_first = WINDOW_Z[SPAN_Z - 1], WINDOW_Z[0]
    lower_there = (at_z > 1, at_z > 0, yes)
    upper_there = (yes, at_z < count_z - 1, at_z < count_z - 2)
    inside_x = (at_x > 0, yes, yes, at_x < count_x - 1)
    inside_z = (at_z > 0, yes, at_z < count_z - 1)
    keep_x = [jnp.where(flag, 1.0, 0.0) for flag in inside_x]
    keep_z = [jnp.where(flag, 1.0, 0.0) for flag in inside_z]
    for z in range(3 * CZ):
        block, i = divmod(z, CZ)
        plain = WINDOW_Z[i + 1]
        scale = float(1.0 / plain)
        if i == 0:
            scale = jnp.where(lower_there[block], float(1.0 / (plain + wz_last)), scale)
        if i == CZ - 1:
            scale = jnp.where(upper_there[block], float(1.0 / (plain + wz_first)), scale)
        for k in range(4):
            blended = extended_ref[z * 32 + k * 8 : z * 32 + k * 8 + 8, :]
            value = 1.0 / (1.0 + jnp.exp(-(blended * (inverse[k] * scale))))
            if block == 1 and k in (1, 2):
                at = i * CX + (k - 1) * 8
                probability_ref[at : at + 8, :] = value
            else:
                value = value * (keep_x[k] * keep_z[block])
            extended_ref[z * 32 + k * 8 : z * 32 + k * 8 + 8, :] = value

    weights = [[taps(radius, degree) for degree in range(3)] for radius in RADII]

    def one_plane(i, carry):
        def plane(offset):
            return extended_ref[pl.ds(pl.multiple_of((i + RIM + offset) * 32, 32), 32), :]

        centre = plane(0)
        results = {}
        for n, radius in enumerate(RADII):
            for degree in (0, 2):
                results[n, degree] = centre * float(weights[n][degree][radius])
        for k in range(1, RIM + 1):
            before, after = plane(-k), plane(k)
            both, change = before + after, before - after
            for n, radius in enumerate(RADII):
                if k > radius:
                    continue
                for degree in range(3):
                    term = (change if degree == 1 else both) * float(weights[n][degree][radius + k])
                    if (n, degree) in results:
                        results[n, degree] = results[n, degree] + term
                    else:
                        results[n, degree] = term
        for n in range(3):
            for degree in range(3):
                upper, lower = two_terms(results[n, degree])
                rows = pl.ds(pl.multiple_of((n * 3 + degree) * 256 + i * 32, 32), 32)
                along_z_ref[rows, 0:YC] = upper
                along_z_ref[rows, YC : 2 * YC] = lower
        return carry

    lax.fori_loop(0, CZ, one_plane, 0)

    total = jnp.zeros((CZ * CX, YC), jnp.float32)
    for n in range(3):
        after_x = {}
        for degree in range(3):
            count = (3 - degree) * 128
            data = along_z_ref[(n * 3 + degree) * 256 : (n * 3 + degree + 1) * 256, :]
            wide = jnp.dot(x_upper_ref[n, :count], data, preferred_element_type=jnp.float32)
            narrow = jnp.dot(
                x_lower_ref[n, :count], data[:, :YC], preferred_element_type=jnp.float32
            )
            summed = wide[:, :YC] + wide[:, YC:] + narrow
            for other in range(3 - degree):
                after_x[degree, other] = summed[other * 128 : (other + 1) * 128]

        def along_y(degree, keys):
            stacked = jnp.concatenate([after_x[key] for key in keys], axis=0)
            pair = jnp.concatenate(two_terms(stacked), axis=1)
            wide = jnp.dot(pair, y_ref[n * 3 + degree], preferred_element_type=jnp.float32)
            summed = wide[:, :YC] + wide[:, YC:]
            return [summed[at * 128 : (at + 1) * 128] for at in range(len(keys))]

        hzz, hxx, hzx = along_y(0, ((2, 0), (0, 2), (1, 1)))
        hzy, hxy = along_y(1, ((1, 0), (0, 1)))
        (hyy,) = along_y(2, ((0, 0),))
        first_inv = hzz + hxx + hyy
        second_inv = hzz * hxx + hzz * hyy + hxx * hyy - hzx * hzx - hzy * hzy - hxy * hxy
        third_inv = (
            hzz * (hxx * hyy - hxy * hxy)
            - hzx * (hzx * hyy - hxy * hzy)
            + hzy * (hzx * hxy - hxx * hzy)
        )
        positive = jnp.maximum(second_inv, 0.0)
        size = jnp.abs(third_inv)
        root = jnp.where(size > 0.0, jnp.exp(jnp.log(size) * (2.0 / 3.0)), 0.0)
        total = total + jnp.maximum(-first_inv, 0.0) * positive / (positive + root + TUBE_FLOOR)
    vessel_ref[...] = VESSEL_GAIN * tissue_ref[...].astype(jnp.float32) * total


def pairs_of(kind, count_z, count_x):
    def flat(z, x):
        return (z % count_z) * count_x + x % count_x

    if kind == "chip":
        return [
            [flat(z, x), flat(z + 1, x)] for z in range(0, count_z, 2) for x in range(count_x)
        ]
    if kind == "slab":
        pairs = [
            [flat(z, x), flat(z + 1, x)] for z in range(1, count_z - 1, 2) for x in range(count_x)
        ]
        return pairs + [
            [flat(z, x), flat(z, x + 1)] for z in (0, count_z - 1) for x in range(0, count_x, 2)
        ]
    pairs = [
        [flat(z, x), flat(z, x + 1)] for z in range(count_z) for x in range(z % 2, count_x - 1, 2)
    ]
    if count_z % 8 == 0:
        idle = [(z, z + 4) for z in range(1, count_z, 2) if z % 8 < 4]
        return pairs + [[flat(z, x), flat(up, x)] for z, up in idle for x in (0, count_x - 1)]
    return pairs + [[flat(z, count_x - 1), flat(z, 0)] for z in range(1, count_z, 2)]


def swap(block, kind):
    groups = pairs_of(kind, lax.axis_size("gz"), lax.axis_size("xy"))
    return lax.all_gather(block, ("gz", "xy"), axis_index_groups=groups, tiled=True)


def whole(count, space=pltpu.VMEM):
    return [pl.BlockSpec(memory_space=space)] * count


def shape_of(*dims):
    return jax.ShapeDtypeStruct(dims, jnp.float32)


def decode(patch_features, conv1_weight, conv1_bias, conv2_weight, conv2_bias, head_weight):
    f32, bf16 = jnp.float32, jnp.bfloat16
    weight_shape = (3, 3, 3, CHANNELS, CHANNELS)
    slots = ((HALF + 2) * SLOT, 2 * YC)
    return pl.pallas_call(
        decoder_kernel,
        out_shape=shape_of(PATCH, YC),
        in_specs=whole(6, pltpu.HBM),
        out_specs=whole(1)[0],
        scratch_shapes=[
            pltpu.VMEM((SPAN_Z, SPAN_X, CHANNELS, YC), bf16),
            pltpu.VMEM(weight_shape, bf16),
            pltpu.VMEM((1, CHANNELS), f32),
            pltpu.VMEM(weight_shape, bf16),
            pltpu.VMEM((1, CHANNELS), f32),
            pltpu.VMEM((1, CHANNELS), bf16),
            pltpu.VMEM(slots, bf16),
            pltpu.VMEM(slots, bf16),
            pltpu.VMEM((ROWS, 3 * SLOT), bf16),
            pltpu.VMEM((ROWS, 3 * SLOT), bf16),
            pltpu.VMEM((ROWS, SPAN_X * YC), bf16),
            pltpu.SemaphoreType.DMA((6,)),
        ],
        compiler_params=pltpu.CompilerParams(vmem_limit_bytes=DECODER_VMEM_LIMIT),
        name="decoder",
    )(
        patch_features.transpose(1, 2, 0, 3),
        conv1_weight.transpose(2, 3, 4, 0, 1),
        conv1_bias.reshape(1, CHANNELS),
        conv2_weight.transpose(2, 3, 4, 0, 1),
        conv2_bias.reshape(1, CHANNELS),
        head_weight.reshape(1, CHANNELS),
    )


def on_device(
    patch_features, conv1_weight, conv1_bias, conv2_weight, conv2_bias, head_weight, tissue_mask
):
    f32, bf16 = jnp.float32, jnp.bfloat16
    params = pltpu.CompilerParams(vmem_limit_bytes=VMEM_LIMIT)
    patch = decode(
        patch_features, conv1_weight, conv1_bias, conv2_weight, conv2_bias, head_weight
    )
    pair = swap(patch, "chip")
    edge = pl.pallas_call(
        edge_kernel,
        out_shape=shape_of(EDGE, YC),
        in_specs=whole(1),
        out_specs=whole(1)[0],
        compiler_params=params,
        name="edge",
    )(pair)
    edges = swap(swap(edge, "x"), "chip")
    chip, send = pl.pallas_call(
        chip_kernel,
        out_shape=(shape_of(CHIP_ROWS * 32, YC), shape_of(SEND_ROWS * 32, YC)),
        in_specs=whole(2),
        out_specs=tuple(whole(2)),
        compiler_params=params,
        name="chip",
    )(pair, edges)
    slabs = swap(send, "slab")
    upper_core = lax.axis_index("gz") & 1
    row_at = jnp.where(upper_core == 1, SEND_ROWS * 32, (SEND_ROWS - 1) * 32)
    rows = swap(lax.dynamic_slice(slabs, (row_at, 0), (32, YC)), "chip")
    x_upper, x_lower, y_all = filter_constants()
    probability, vesselness = pl.pallas_call(
        vessel_kernel,
        out_shape=(shape_of(CZ * CX, YC), shape_of(CZ * CX, YC)),
        in_specs=whole(7),
        out_specs=tuple(whole(2)),
        scratch_shapes=[
            pltpu.VMEM((3 * CZ * 32, YC), f32),
            pltpu.VMEM((9 * 256, 2 * YC), bf16),
        ],
        compiler_params=params,
        name="vessel",
    )(
        chip,
        slabs,
        rows,
        tissue_mask.reshape(CZ * CX, YC),
        jnp.asarray(x_upper),
        jnp.asarray(x_lower),
        jnp.asarray(y_all),
    )
    return (
        probability.reshape(CZ, CX, YC),
        vesselness.reshape(CZ, CX, YC),
    )


def solution(mesh):
    placed = (P(None, "gz", "xy", None), P(), P(), P(), P(), P(), P("gz", "xy", None))
    return jax.shard_map(
        on_device,
        mesh=mesh,
        in_specs=placed,
        out_specs=(P("gz", "xy", None), P("gz", "xy", None)),
        check_vma=False,
    )
```

```python
import jax
import jax.numpy as jnp
import numpy as np
from jax import lax
from jax.experimental import pallas as pl
from jax.experimental.pallas import tpu as pltpu
from jax.sharding import PartitionSpec as P

CHANNELS = 16
CZ = 8
CX = 16
YC = 128
MARGIN = 1
RIM = 8
SPAN_Z = CZ + 2 * MARGIN
SPAN_X = CX + 2 * MARGIN
HALF = SPAN_X // 2
ROWS = SPAN_Z * CHANNELS
SLOT = ROWS + 3 * CHANNELS
REACH = 5 * CHANNELS
BLOCKS = ((0, 3), (3, 3), (6, 2), (8, 2))
RADII = (RIM // 4, RIM // 2, RIM)
VESSEL_GAIN = 4.0
TUBE_FLOOR = 0.01
PATCH = SPAN_Z * CX + 2 * 16
CHIP_ROWS = 2 * CZ + 2
EDGE = 168
SEND_ROWS = CHIP_ROWS // 2
VMEM_LIMIT = 24 * 1024 * 1024
DECODER_VMEM_LIMIT = 63 * 1024 * 1024


def window(size):
    position = np.arange(size, dtype=np.float64)
    return np.exp(-0.5 * ((position - (size - 1) / 2.0) / (size / 4.0)) ** 2)


WINDOW_Z = window(SPAN_Z)
WINDOW_X = window(SPAN_X)


def taps(radius, degree):
    spread = radius / 3.0
    offsets = np.arange(-radius, radius + 1, dtype=np.float64)
    gaussian = np.exp(-offsets * offsets / (2.0 * spread * spread))
    gaussian = gaussian / gaussian.sum()
    if degree == 1:
        return -offsets / spread**2 * gaussian
    if degree == 2:
        return (offsets**2 / spread**4 - 1.0 / spread**2) * gaussian
    return gaussian


def band(out_len, in_len, offset, radius, degree):
    weights = taps(radius, degree)
    distance = np.arange(out_len)[:, None] + offset - np.arange(in_len)[None, :]
    inside = np.abs(distance) <= radius
    return np.where(inside, weights[np.clip(distance, -radius, radius) + radius], 0.0)


def split_terms(matrix):
    whole = matrix.astype(np.float32)
    upper = whole.astype(jnp.bfloat16)
    lower = (whole - upper.astype(np.float32)).astype(jnp.bfloat16)
    return upper, lower


def filter_constants():
    x_all, y_all = [], []
    for radius in RADII:
        blocks = [band(CX, CX + 2 * RIM, RIM, radius, degree) for degree in range(3)]
        upper, lower = split_terms(np.concatenate(blocks, axis=0))
        x_all.append(np.concatenate([upper, upper, lower], axis=1))
        for degree in range(3):
            scaled = (radius / 3.0) ** 2 * band(YC, YC, 0, radius, degree).T
            upper, lower = split_terms(scaled)
            top = np.concatenate([upper, lower], axis=1)
            bottom = np.concatenate([upper, np.zeros_like(lower)], axis=1)
            y_all.append(np.concatenate([top, bottom], axis=0))
    return np.stack(x_all), np.stack(y_all)


def iota(shape, dim):
    return lax.broadcasted_iota(jnp.int32, shape, dim)


def sum_over_y(parts):
    lane = iota(parts[0].shape, 1)
    before = jnp.where(lane == 0, 0.0, pltpu.roll(parts[0], 1, 1))
    after = jnp.where(lane == YC - 1, 0.0, pltpu.roll(parts[2], YC - 1, 1))
    return before + parts[1] + after


def store_part(slots_ref, slot, half, z, part):
    at = slot * SLOT + (z + 1) * CHANNELS
    slots_ref[at : at + part.shape[0], half * YC : (half + 1) * YC] = part


def expand_weight(weight_ref, wide_ref):
    shape = (CHANNELS, 3 * REACH)
    lane = iota(shape, 1)
    group = (lane >= REACH).astype(jnp.int32) + (lane >= 2 * REACH).astype(jnp.int32)
    same = (lane & (CHANNELS - 1)) == iota(shape, 0)
    spread = jnp.zeros((9 * CHANNELS, 3 * REACH), jnp.float32)
    for dx in range(3):
        pick = jnp.where(same & (group == dx), 1.0, 0.0).astype(jnp.bfloat16)
        part = weight_ref[:, dx].reshape(9 * CHANNELS, CHANNELS)
        spread = spread + jnp.dot(part, pick, preferred_element_type=jnp.float32)
    plane = (lane - group * REACH) >> 4
    for z in range(3):
        for dy in range(3):
            rows = jnp.zeros(shape, jnp.float32)
            for dz in range(3):
                at = (dz * 3 + dy) * CHANNELS
                rows = jnp.where(plane == z + dz, spread[at : at + CHANNELS], rows)
            at = (z * 3 + dy) * CHANNELS
            wide_ref[at : at + CHANNELS, :] = rows.astype(jnp.bfloat16)


def column_of(row_ref):
    eye = iota((CHANNELS, CHANNELS), 0) == iota((CHANNELS, CHANNELS), 1)
    row = row_ref[...].astype(jnp.float32)
    return jnp.sum(jnp.where(eye, row, 0.0), axis=1, keepdims=True)


def decoder_kernel(
    features_hbm,
    weight1_hbm,
    bias1_hbm,
    weight2_hbm,
    bias2_hbm,
    head_hbm,
    patch_ref,
    features_ref,
    weight1_ref,
    bias1_ref,
    weight2_ref,
    bias2_ref,
    head_ref,
    first_ref,
    second_ref,
    wide1_ref,
    wide2_ref,
    last_ref,
    arrived,
):
    routes = (
        (weight1_hbm, weight1_ref),
        (weight2_hbm, weight2_ref),
        (bias1_hbm, bias1_ref),
        (bias2_hbm, bias2_ref),
        (head_hbm, head_ref),
        (features_hbm, features_ref),
    )
    copies = [
        pltpu.make_async_copy(source, target, arrived.at[k])
        for k, (source, target) in enumerate(routes)
    ]
    for copy in copies:
        copy.start()
    for ref in (first_ref, second_ref):
        ref[0:SLOT, 0:YC] = jnp.zeros((SLOT, YC), jnp.bfloat16)
        ref[(HALF + 1) * SLOT :, YC:] = jnp.zeros((SLOT, YC), jnp.bfloat16)
        for slot in range(HALF + 2):
            base = slot * SLOT
            ref[base : base + CHANNELS, :] = jnp.zeros((CHANNELS, 2 * YC), jnp.bfloat16)
            ref[base + CHANNELS + ROWS : base + SLOT, :] = jnp.zeros(
                (2 * CHANNELS, 2 * YC), jnp.bfloat16
            )
    copies[0].wait()
    expand_weight(weight1_ref, wide1_ref)
    copies[1].wait()
    expand_weight(weight2_ref, wide2_ref)
    for copy in copies[2:]:
        copy.wait()
    for x in range(SPAN_X):
        column = features_ref[:, x].reshape(ROWS, YC)
        if x <= HALF:
            store_part(first_ref, x + 1, 0, 0, column)
        if x >= HALF - 1:
            store_part(first_ref, x - HALF + 1, 1, 0, column)

    def layer(wide_ref, slots_ref, bias, step, put):
        for first, count in BLOCKS:
            pieces = []
            for dx in range(3):
                at = (step + dx) * SLOT + first * CHANNELS
                pieces.append(slots_ref[at : at + REACH, :])
            summed = jnp.dot(
                wide_ref[: count * 3 * CHANNELS],
                jnp.concatenate(pieces, axis=0),
                preferred_element_type=jnp.float32,
            )
            for z in range(count):
                for half in range(2):
                    parts = []
                    for dy in range(3):
                        at = (z * 3 + dy) * CHANNELS
                        parts.append(summed[at : at + CHANNELS, half * YC : (half + 1) * YC])
                    value = jnp.maximum(sum_over_y(parts) + bias, 0.0)
                    put(first + z, half, value.astype(jnp.bfloat16))

    bias1 = column_of(bias1_ref)
    for step in range(HALF):

        def put_first(z, half, part, step=step):
            store_part(second_ref, step + 1, half, z, part)
            if half == 0 and step == HALF - 1:
                store_part(second_ref, 0, 1, z, part)
            if half == 1 and step == 0:
                store_part(second_ref, HALF + 1, 0, z, part)

        layer(wide1_ref, first_ref, bias1, step, put_first)

    bias2 = column_of(bias2_ref)
    repeat = ((iota((CHANNELS, ROWS), 1) & (CHANNELS - 1)) == iota((CHANNELS, ROWS), 0)).astype(
        jnp.float32
    )
    head_lanes = jnp.sum(
        repeat * column_of(head_ref), axis=0, keepdims=True
    )
    head = jnp.where(
        (iota((16, ROWS), 1) >> 4) == iota((16, ROWS), 0), head_lanes, 0.0
    ).astype(jnp.bfloat16)
    place = iota((16, YC), 0).astype(jnp.float32)
    centred = (place - (SPAN_Z - 1) / 2.0) / (SPAN_Z / 4.0)
    weight_z = jnp.exp(-0.5 * centred * centred)
    for step in range(HALF):

        def put_last(z, half, part, step=step):
            at = (step * 2 + half) * YC
            last_ref[z * CHANNELS : (z + 1) * CHANNELS, at : at + YC] = part

        layer(wide2_ref, second_ref, bias2, step, put_last)
    logits = jnp.dot(head, last_ref[...], preferred_element_type=jnp.float32)
    for step in range(HALF):
        for half in range(2):
            x = step + half * HALF
            at = (step * 2 + half) * YC
            weighted = logits[:, at : at + YC] * (weight_z * float(WINDOW_X[x]))
            if x == 0 or x == SPAN_X - 1:
                side = 0 if x == 0 else 1
                patch_ref[160 + side * 16 : 176 + side * 16, :] = weighted
            else:
                patch_ref[pl.ds(x - 1, SPAN_Z, stride=CX), :] = weighted[:SPAN_Z]


def chip_row(pair_ref, r):
    low, high = r + 1, r - CZ + 1
    value = None
    for patch, index in ((0, low), (1, high)):
        if 0 <= index < SPAN_Z:
            base = patch * PATCH + index * CX
            part = pair_ref[base : base + CX, :]
            value = part if value is None else value + part
    return value


def chip_margin(pair_ref, side, r):
    low, high = r + 1, r - CZ + 1
    value = None
    for patch, index in ((0, low), (1, high)):
        if 0 <= index < SPAN_Z:
            base = patch * PATCH + SPAN_Z * CX + side * 16 + index
            part = pair_ref[base : base + 1, :]
            value = part if value is None else value + part
    return value


def position():
    return lax.axis_index("gz"), lax.axis_size("gz"), lax.axis_index("xy"), lax.axis_size("xy")


def edge_kernel(pair_ref, edge_ref):
    at_z, _, at_x, _ = position()
    to_right = ((at_z + at_x) & 1) == 0
    for n in range(CHIP_ROWS):
        value = chip_row(pair_ref, n - 1)
        edge_ref[n * 8 : (n + 1) * 8, :] = jnp.where(to_right, value[8:], value[:8])
        left, right = (chip_margin(pair_ref, side, n - 1) for side in range(2))
        edge_ref[CHIP_ROWS * 8 + n : CHIP_ROWS * 8 + n + 1, :] = jnp.where(to_right, right, left)
    edge_ref[CHIP_ROWS * 9 :, :] = jnp.zeros((EDGE - CHIP_ROWS * 9, YC), jnp.float32)


def chip_kernel(pair_ref, edges_ref, chip_ref, send_ref):
    at_z, _, at_x, count_x = position()
    odd_x = at_x & 1
    from_left = (1 - odd_x) * (2 * EDGE)
    from_right = odd_x * (2 * EDGE) + EDGE
    sub = iota((8, YC), 0)
    has_left = jnp.where(at_x > 0, 1.0, 0.0)
    has_right = jnp.where(at_x < count_x - 1, 1.0, 0.0)
    upper_core = (at_z & 1) == 1

    def part(start, offset, count):
        return edges_ref[pl.ds(pl.multiple_of(start, 8) + offset, count), :]

    left_margins = [part(from_left, CHIP_ROWS * 8 + 8 * n, 8) * has_left for n in range(3)]
    right_margins = [part(from_right, CHIP_ROWS * 8 + 8 * n, 8) * has_right for n in range(3)]
    for n in range(CHIP_ROWS):
        own = chip_row(pair_ref, n - 1)
        first_margin, last_margin = (chip_margin(pair_ref, side, n - 1) for side in range(2))
        block, at = divmod(n, 8)
        left_margin = left_margins[block][at : at + 1]
        right_margin = right_margins[block][at : at + 1]
        sums = (
            part(from_left, n * 8, 8) * has_left + jnp.where(sub == 7, first_margin, 0.0),
            own[:8] + jnp.where(sub == 0, left_margin, 0.0),
            own[8:] + jnp.where(sub == 7, right_margin, 0.0),
            part(from_right, n * 8, 8) * has_right + jnp.where(sub == 0, last_margin, 0.0),
        )
        for k in range(4):
            at = n * 32 + k * 8
            chip_ref[at : at + 8, :] = sums[k]
            low = k * 8 + n * 32
            high = k * 8 + (n - SEND_ROWS) * 32
            if n < SEND_ROWS:

                @pl.when(jnp.logical_not(upper_core))
                def _(value=sums[k], low=low):
                    send_ref[low : low + 8, :] = value

            else:

                @pl.when(upper_core)
                def _(value=sums[k], high=high):
                    send_ref[high : high + 8, :] = value


def two_terms(values):
    upper = values.astype(jnp.bfloat16)
    lower = (values - upper.astype(jnp.float32)).astype(jnp.bfloat16)
    return upper, lower


def vessel_kernel(
    chip_ref,
    slabs_ref,
    rows_ref,
    tissue_ref,
    x_ref,
    y_ref,
    probability_ref,
    vessel_ref,
    extended_ref,
    along_z_ref,
):
    at_z, count_z, at_x, count_x = position()
    upper_core = (at_z & 1) == 1
    below = jnp.where(at_z - (at_z & 1) > 0, 1.0, 0.0)
    above = jnp.where(at_z - (at_z & 1) < count_z - 2, 1.0, 0.0)

    @pl.when(jnp.logical_not(upper_core))
    def _():
        for z in range(3 * CZ):
            value = None
            if z >= RIM - 1:
                n = z - RIM + 1
                value = chip_ref[n * 32 : (n + 1) * 32, :]
            if z < SEND_ROWS:
                part = slabs_ref[z * 32 : (z + 1) * 32, :] * below
                value = part if value is None else value + part
            if z == 3 * CZ - 1:
                value = value + rows_ref[32:64, :] * above
            extended_ref[z * 32 : (z + 1) * 32, :] = value

    @pl.when(upper_core)
    def _():
        for z in range(3 * CZ):
            value = None
            if z + 1 < CHIP_ROWS:
                value = chip_ref[(z + 1) * 32 : (z + 2) * 32, :]
            if z >= 3 * CZ - SEND_ROWS:
                n = SEND_ROWS + z - (3 * CZ - SEND_ROWS)
                part = slabs_ref[n * 32 : (n + 1) * 32, :] * above
                value = part if value is None else value + part
            if z == 0:
                value = value + rows_ref[0:32, :] * below
            extended_ref[z * 32 : (z + 1) * 32, :] = value

    sub = iota((8, YC), 0)

    def inverse_x(first, edge, edge_row, present):
        cover = jnp.zeros((8, YC), jnp.float32)
        for j in range(8):
            cover = jnp.where(sub == j, float(WINDOW_X[first + j + 1]), cover)
        extra = jnp.where(present, float(edge), 0.0)
        return 1.0 / (cover + jnp.where(sub == edge_row, extra, 0.0))

    wx_last, wx_first = WINDOW_X[SPAN_X - 1], WINDOW_X[0]
    yes = at_x >= 0
    inverse = [
        inverse_x(8, wx_first, 7, yes),
        inverse_x(0, wx_last, 0, at_x > 0),
        inverse_x(8, wx_first, 7, at_x < count_x - 1),
        inverse_x(0, wx_last, 0, yes),
    ]
    wz_last, wz_first = WINDOW_Z[SPAN_Z - 1], WINDOW_Z[0]
    lower_there = (at_z > 1, at_z > 0, yes)
    upper_there = (yes, at_z < count_z - 1, at_z < count_z - 2)
    inside_x = (at_x > 0, yes, yes, at_x < count_x - 1)
    inside_z = (at_z > 0, yes, at_z < count_z - 1)
    keep_x = [jnp.where(flag, 1.0, 0.0) for flag in inside_x]
    keep_z = [jnp.where(flag, 1.0, 0.0) for flag in inside_z]
    for z in range(3 * CZ):
        block, i = divmod(z, CZ)
        plain = WINDOW_Z[i + 1]
        scale = float(1.0 / plain)
        if i == 0:
            scale = jnp.where(lower_there[block], float(1.0 / (plain + wz_last)), scale)
        if i == CZ - 1:
            scale = jnp.where(upper_there[block], float(1.0 / (plain + wz_first)), scale)
        for k in range(4):
            blended = extended_ref[z * 32 + k * 8 : z * 32 + k * 8 + 8, :]
            value = 1.0 / (1.0 + jnp.exp(-(blended * (inverse[k] * scale))))
            if block == 1 and k in (1, 2):
                at = i * CX + (k - 1) * 8
                probability_ref[at : at + 8, :] = value
            else:
                value = value * (keep_x[k] * keep_z[block])
            extended_ref[z * 32 + k * 8 : z * 32 + k * 8 + 8, :] = value

    weights = [[taps(radius, degree) for degree in range(3)] for radius in RADII]

    def filter_z(n, radius):
        for i in range(CZ):

            def plane(offset):
                at = (i + RIM + offset) * 32
                return extended_ref[at : at + 32, :]

            centre = plane(0)
            results = [centre * float(weights[n][degree][radius]) for degree in range(3)]
            for k in range(1, radius + 1):
                before, after = plane(-k), plane(k)
                both, change = before + after, before - after
                for degree in range(3):
                    term = (change if degree == 1 else both) * float(weights[n][degree][radius + k])
                    fresh = degree == 1 and k == 1
                    results[degree] = term if fresh else results[degree] + term
            for degree in range(3):
                upper, lower = two_terms(results[degree])
                base = (n * 3 + degree) * 96
                for at, part in ((0, upper), (32, lower), (64, upper)):
                    along_z_ref[base + at : base + at + 32, i * YC : (i + 1) * YC] = part

    total = jnp.zeros((CZ * CX, YC), jnp.float32)
    filter_z(0, RADII[0])
    for n in range(3):
        if n < 2:
            filter_z(n + 1, RADII[n + 1])
        after_x = {}
        for degree in range(3):
            data = along_z_ref[(n * 3 + degree) * 96 : (n * 3 + degree + 1) * 96, :]
            wide = jnp.dot(
                x_ref[n, : (3 - degree) * CX], data, preferred_element_type=jnp.float32
            )
            for other in range(3 - degree):
                rows = wide[other * CX : (other + 1) * CX]
                after_x[degree, other] = jnp.concatenate(
                    [rows[:, z * YC : (z + 1) * YC] for z in range(CZ)], axis=0
                )

        def along_y(degree, keys):
            stacked = jnp.concatenate([after_x[key] for key in keys], axis=0)
            pair = jnp.concatenate(two_terms(stacked), axis=1)
            wide = jnp.dot(pair, y_ref[n * 3 + degree], preferred_element_type=jnp.float32)
            summed = wide[:, :YC] + wide[:, YC:]
            return [summed[at * 128 : (at + 1) * 128] for at in range(len(keys))]

        hzz, hxx, hzx = along_y(0, ((2, 0), (0, 2), (1, 1)))
        hzy, hxy = along_y(1, ((1, 0), (0, 1)))
        (hyy,) = along_y(2, ((0, 0),))
        first_inv = hzz + hxx + hyy
        second_inv = hzz * hxx + hzz * hyy + hxx * hyy - hzx * hzx - hzy * hzy - hxy * hxy
        third_inv = (
            hzz * (hxx * hyy - hxy * hxy)
            - hzx * (hzx * hyy - hxy * hzy)
            + hzy * (hzx * hxy - hxx * hzy)
        )
        positive = jnp.maximum(second_inv, 0.0)
        size = jnp.abs(third_inv)
        root = jnp.where(size > 0.0, jnp.exp(jnp.log(size) * (2.0 / 3.0)), 0.0)
        total = total + jnp.maximum(-first_inv, 0.0) * positive / (positive + root + TUBE_FLOOR)
    vessel_ref[...] = VESSEL_GAIN * tissue_ref[...].astype(jnp.float32) * total


def pairs_of(kind, count_z, count_x):
    def flat(z, x):
        return (z % count_z) * count_x + x % count_x

    if kind == "chip":
        return [
            [flat(z, x), flat(z + 1, x)] for z in range(0, count_z, 2) for x in range(count_x)
        ]
    if kind == "slab":
        pairs = [
            [flat(z, x), flat(z + 1, x)] for z in range(1, count_z - 1, 2) for x in range(count_x)
        ]
        return pairs + [
            [flat(z, x), flat(z, x + 1)] for z in (0, count_z - 1) for x in range(0, count_x, 2)
        ]
    pairs = [
        [flat(z, x), flat(z, x + 1)] for z in range(count_z) for x in range(z % 2, count_x - 1, 2)
    ]
    if count_z % 8 == 0:
        idle = [(z, z + 4) for z in range(1, count_z, 2) if z % 8 < 4]
        return pairs + [[flat(z, x), flat(up, x)] for z, up in idle for x in (0, count_x - 1)]
    return pairs + [[flat(z, count_x - 1), flat(z, 0)] for z in range(1, count_z, 2)]


def swap(block, kind):
    groups = pairs_of(kind, lax.axis_size("gz"), lax.axis_size("xy"))
    return lax.all_gather(block, ("gz", "xy"), axis_index_groups=groups, tiled=True)


def whole(count, space=pltpu.VMEM):
    return [pl.BlockSpec(memory_space=space)] * count


def shape_of(*dims):
    return jax.ShapeDtypeStruct(dims, jnp.float32)


def decode(patch_features, conv1_weight, conv1_bias, conv2_weight, conv2_bias, head_weight):
    f32, bf16 = jnp.float32, jnp.bfloat16
    weight_shape = (3, 3, 3, CHANNELS, CHANNELS)
    slots = ((HALF + 2) * SLOT, 2 * YC)
    return pl.pallas_call(
        decoder_kernel,
        out_shape=shape_of(PATCH, YC),
        in_specs=whole(6, pltpu.HBM),
        out_specs=whole(1)[0],
        scratch_shapes=[
            pltpu.VMEM((SPAN_Z, SPAN_X, CHANNELS, YC), bf16),
            pltpu.VMEM(weight_shape, bf16),
            pltpu.VMEM((1, CHANNELS), f32),
            pltpu.VMEM(weight_shape, bf16),
            pltpu.VMEM((1, CHANNELS), f32),
            pltpu.VMEM((1, CHANNELS), bf16),
            pltpu.VMEM(slots, bf16),
            pltpu.VMEM(slots, bf16),
            pltpu.VMEM((9 * CHANNELS, 3 * REACH), bf16),
            pltpu.VMEM((9 * CHANNELS, 3 * REACH), bf16),
            pltpu.VMEM((ROWS, SPAN_X * YC), bf16),
            pltpu.SemaphoreType.DMA((6,)),
        ],
        compiler_params=pltpu.CompilerParams(vmem_limit_bytes=DECODER_VMEM_LIMIT),
        name="decoder",
    )(
        patch_features.transpose(1, 2, 0, 3),
        conv1_weight.transpose(2, 3, 4, 0, 1),
        conv1_bias.reshape(1, CHANNELS),
        conv2_weight.transpose(2, 3, 4, 0, 1),
        conv2_bias.reshape(1, CHANNELS),
        head_weight.reshape(1, CHANNELS),
    )


def measure_tubes(chip, slabs, rows, tissue_mask):
    f32, bf16 = jnp.float32, jnp.bfloat16
    params = pltpu.CompilerParams(vmem_limit_bytes=VMEM_LIMIT)
    x_all, y_all = filter_constants()
    return pl.pallas_call(
        vessel_kernel,
        out_shape=(shape_of(CZ * CX, YC), shape_of(CZ * CX, YC)),
        in_specs=whole(6),
        out_specs=tuple(whole(2)),
        scratch_shapes=[
            pltpu.VMEM((3 * CZ * 32, YC), f32),
            pltpu.VMEM((9 * 96, CZ * YC), bf16),
        ],
        compiler_params=params,
        name="vessel",
    )(
        chip,
        slabs,
        rows,
        tissue_mask.reshape(CZ * CX, YC),
        jnp.asarray(x_all),
        jnp.asarray(y_all),
    )


def on_device(
    patch_features, conv1_weight, conv1_bias, conv2_weight, conv2_bias, head_weight, tissue_mask
):
    params = pltpu.CompilerParams(vmem_limit_bytes=VMEM_LIMIT)
    patch = decode(
        patch_features, conv1_weight, conv1_bias, conv2_weight, conv2_bias, head_weight
    )
    pair = swap(patch, "chip")
    edge = pl.pallas_call(
        edge_kernel,
        out_shape=shape_of(EDGE, YC),
        in_specs=whole(1),
        out_specs=whole(1)[0],
        compiler_params=params,
        name="edge",
    )(pair)
    edges = swap(swap(edge, "x"), "chip")
    chip, send = pl.pallas_call(
        chip_kernel,
        out_shape=(shape_of(CHIP_ROWS * 32, YC), shape_of(SEND_ROWS * 32, YC)),
        in_specs=whole(2),
        out_specs=tuple(whole(2)),
        compiler_params=params,
        name="chip",
    )(pair, edges)
    slabs = swap(send, "slab")
    upper_core = lax.axis_index("gz") & 1
    row_at = jnp.where(upper_core == 1, SEND_ROWS * 32, (SEND_ROWS - 1) * 32)
    rows = swap(lax.dynamic_slice(slabs, (row_at, 0), (32, YC)), "chip")
    probability, vesselness = measure_tubes(chip, slabs, rows, tissue_mask)
    return (
        probability.reshape(CZ, CX, YC),
        vesselness.reshape(CZ, CX, YC),
    )


def solution(mesh):
    placed = (P(None, "gz", "xy", None), P(), P(), P(), P(), P(), P("gz", "xy", None))
    return jax.shard_map(
        on_device,
        mesh=mesh,
        in_specs=placed,
        out_specs=(P("gz", "xy", None), P("gz", "xy", None)),
        check_vma=False,
    )
```

```python
import jax
import jax.numpy as jnp
import numpy as np
from jax import lax
from jax.experimental import pallas as pl
from jax.experimental.pallas import tpu as pltpu
from jax.sharding import PartitionSpec as P

CHANNELS = 16
CZ = 8
CX = 16
YC = 128
MARGIN = 1
RIM = 8
SPAN_Z = CZ + 2 * MARGIN
SPAN_X = CX + 2 * MARGIN
HALF = SPAN_X // 2
ROWS = SPAN_Z * CHANNELS
SLOT = ROWS + 3 * CHANNELS
REACH = 5 * CHANNELS
BLOCKS = ((0, 3), (3, 3), (6, 2), (8, 2))
RADII = (RIM // 4, RIM // 2, RIM)
VESSEL_GAIN = 4.0
TUBE_FLOOR = 0.01
PATCH = SPAN_Z * CX + 2 * 16
CHIP_ROWS = 2 * CZ + 2
EDGE = 168
SEND_ROWS = CHIP_ROWS // 2
VMEM_LIMIT = 24 * 1024 * 1024
DECODER_VMEM_LIMIT = 63 * 1024 * 1024


def window(size):
    position = np.arange(size, dtype=np.float64)
    return np.exp(-0.5 * ((position - (size - 1) / 2.0) / (size / 4.0)) ** 2)


WINDOW_Z = window(SPAN_Z)
WINDOW_X = window(SPAN_X)


def taps(radius, degree):
    spread = radius / 3.0
    offsets = np.arange(-radius, radius + 1, dtype=np.float64)
    gaussian = np.exp(-offsets * offsets / (2.0 * spread * spread))
    gaussian = gaussian / gaussian.sum()
    if degree == 1:
        return -offsets / spread**2 * gaussian
    if degree == 2:
        return (offsets**2 / spread**4 - 1.0 / spread**2) * gaussian
    return gaussian


def band(out_len, in_len, offset, radius, degree):
    weights = taps(radius, degree)
    distance = np.arange(out_len)[:, None] + offset - np.arange(in_len)[None, :]
    inside = np.abs(distance) <= radius
    return np.where(inside, weights[np.clip(distance, -radius, radius) + radius], 0.0)


def split_terms(matrix):
    whole = matrix.astype(np.float32)
    upper = whole.astype(jnp.bfloat16)
    lower = (whole - upper.astype(np.float32)).astype(jnp.bfloat16)
    return upper, lower


def filter_constants():
    x_all, y_all = [], []
    for radius in RADII:
        blocks = [band(CX, CX + 2 * RIM, RIM, radius, degree) for degree in range(3)]
        upper, lower = split_terms(np.concatenate(blocks, axis=0))
        x_all.append(np.concatenate([upper, upper, lower], axis=1))
        for degree in range(3):
            scaled = (radius / 3.0) ** 2 * band(YC, YC, 0, radius, degree).T
            upper, lower = split_terms(scaled)
            top = np.concatenate([upper, lower], axis=1)
            bottom = np.concatenate([upper, np.zeros_like(lower)], axis=1)
            y_all.append(np.concatenate([top, bottom], axis=0))
    return np.stack(x_all), np.stack(y_all)


def iota(shape, dim):
    return lax.broadcasted_iota(jnp.int32, shape, dim)


def sum_over_y(parts):
    lane = iota(parts[0].shape, 1)
    before = jnp.where(lane == 0, 0.0, pltpu.roll(parts[0], 1, 1))
    after = jnp.where(lane == YC - 1, 0.0, pltpu.roll(parts[2], YC - 1, 1))
    return before + parts[1] + after


def store_part(slots_ref, slot, half, z, part):
    at = slot * SLOT + (z + 1) * CHANNELS
    slots_ref[at : at + part.shape[0], half * YC : (half + 1) * YC] = part


def expand_weight(weight_ref, wide_ref):
    shape = (CHANNELS, 3 * REACH)
    lane = iota(shape, 1)
    group = (lane >= REACH).astype(jnp.int32) + (lane >= 2 * REACH).astype(jnp.int32)
    same = (lane & (CHANNELS - 1)) == iota(shape, 0)
    spread = jnp.zeros((9 * CHANNELS, 3 * REACH), jnp.float32)
    for dx in range(3):
        pick = jnp.where(same & (group == dx), 1.0, 0.0).astype(jnp.bfloat16)
        part = weight_ref[:, dx].reshape(9 * CHANNELS, CHANNELS)
        spread = spread + jnp.dot(part, pick, preferred_element_type=jnp.float32)
    plane = (lane - group * REACH) >> 4
    for z in range(3):
        for dy in range(3):
            rows = jnp.zeros(shape, jnp.float32)
            for dz in range(3):
                at = (dz * 3 + dy) * CHANNELS
                rows = jnp.where(plane == z + dz, spread[at : at + CHANNELS], rows)
            at = (z * 3 + dy) * CHANNELS
            wide_ref[at : at + CHANNELS, :] = rows.astype(jnp.bfloat16)


def column_of(row_ref):
    eye = iota((CHANNELS, CHANNELS), 0) == iota((CHANNELS, CHANNELS), 1)
    row = row_ref[...].astype(jnp.float32)
    return jnp.sum(jnp.where(eye, row, 0.0), axis=1, keepdims=True)


def decoder_kernel(
    features_hbm,
    weight1_hbm,
    bias1_hbm,
    weight2_hbm,
    bias2_hbm,
    head_hbm,
    patch_ref,
    features_ref,
    weight1_ref,
    bias1_ref,
    weight2_ref,
    bias2_ref,
    head_ref,
    first_ref,
    second_ref,
    wide1_ref,
    wide2_ref,
    last_ref,
    arrived,
):
    routes = (
        (weight1_hbm, weight1_ref),
        (weight2_hbm, weight2_ref),
        (bias1_hbm, bias1_ref),
        (bias2_hbm, bias2_ref),
        (head_hbm, head_ref),
        (features_hbm, features_ref),
    )
    copies = [
        pltpu.make_async_copy(source, target, arrived.at[k])
        for k, (source, target) in enumerate(routes)
    ]
    for copy in copies:
        copy.start()
    for ref in (first_ref, second_ref):
        ref[0:SLOT, 0:YC] = jnp.zeros((SLOT, YC), jnp.bfloat16)
        ref[(HALF + 1) * SLOT :, YC:] = jnp.zeros((SLOT, YC), jnp.bfloat16)
        for slot in range(HALF + 2):
            base = slot * SLOT
            ref[base : base + CHANNELS, :] = jnp.zeros((CHANNELS, 2 * YC), jnp.bfloat16)
            ref[base + CHANNELS + ROWS : base + SLOT, :] = jnp.zeros(
                (2 * CHANNELS, 2 * YC), jnp.bfloat16
            )
    copies[0].wait()
    expand_weight(weight1_ref, wide1_ref)
    copies[1].wait()
    expand_weight(weight2_ref, wide2_ref)
    for copy in copies[2:]:
        copy.wait()
    for x in range(SPAN_X):
        column = features_ref[:, x].reshape(ROWS, YC)
        if x <= HALF:
            store_part(first_ref, x + 1, 0, 0, column)
        if x >= HALF - 1:
            store_part(first_ref, x - HALF + 1, 1, 0, column)

    def layer(wide_ref, slots_ref, bias, step, put):
        for first, count in BLOCKS:
            pieces = []
            for dx in range(3):
                at = (step + dx) * SLOT + first * CHANNELS
                pieces.append(slots_ref[at : at + REACH, :])
            summed = jnp.dot(
                wide_ref[: count * 3 * CHANNELS],
                jnp.concatenate(pieces, axis=0),
                preferred_element_type=jnp.float32,
            )
            for z in range(count):
                for half in range(2):
                    parts = []
                    for dy in range(3):
                        at = (z * 3 + dy) * CHANNELS
                        parts.append(summed[at : at + CHANNELS, half * YC : (half + 1) * YC])
                    value = jnp.maximum(sum_over_y(parts) + bias, 0.0)
                    put(first + z, half, value.astype(jnp.bfloat16))

    bias1 = column_of(bias1_ref)
    for step in range(HALF):

        def put_first(z, half, part, step=step):
            store_part(second_ref, step + 1, half, z, part)
            if half == 0 and step == HALF - 1:
                store_part(second_ref, 0, 1, z, part)
            if half == 1 and step == 0:
                store_part(second_ref, HALF + 1, 0, z, part)

        layer(wide1_ref, first_ref, bias1, step, put_first)

    bias2 = column_of(bias2_ref)
    repeat = ((iota((CHANNELS, ROWS), 1) & (CHANNELS - 1)) == iota((CHANNELS, ROWS), 0)).astype(
        jnp.float32
    )
    head_lanes = jnp.sum(
        repeat * column_of(head_ref), axis=0, keepdims=True
    )
    head = jnp.where(
        (iota((16, ROWS), 1) >> 4) == iota((16, ROWS), 0), head_lanes, 0.0
    ).astype(jnp.bfloat16)
    place = iota((16, YC), 0).astype(jnp.float32)
    centred = (place - (SPAN_Z - 1) / 2.0) / (SPAN_Z / 4.0)
    weight_z = jnp.exp(-0.5 * centred * centred)
    for step in range(HALF):

        def put_last(z, half, part, step=step):
            at = (step * 2 + half) * YC
            last_ref[z * CHANNELS : (z + 1) * CHANNELS, at : at + YC] = part

        layer(wide2_ref, second_ref, bias2, step, put_last)
    logits = jnp.dot(head, last_ref[...], preferred_element_type=jnp.float32)
    for step in range(HALF):
        for half in range(2):
            x = step + half * HALF
            at = (step * 2 + half) * YC
            weighted = logits[:, at : at + YC] * (weight_z * float(WINDOW_X[x]))
            if x == 0 or x == SPAN_X - 1:
                side = 0 if x == 0 else 1
                patch_ref[160 + side * 16 : 176 + side * 16, :] = weighted
            else:
                patch_ref[pl.ds(x - 1, SPAN_Z, stride=CX), :] = weighted[:SPAN_Z]


def chip_row(pair_ref, r):
    low, high = r + 1, r - CZ + 1
    value = None
    for patch, index in ((0, low), (1, high)):
        if 0 <= index < SPAN_Z:
            base = patch * PATCH + index * CX
            part = pair_ref[base : base + CX, :]
            value = part if value is None else value + part
    return value


def chip_margin(pair_ref, side, r):
    low, high = r + 1, r - CZ + 1
    value = None
    for patch, index in ((0, low), (1, high)):
        if 0 <= index < SPAN_Z:
            base = patch * PATCH + SPAN_Z * CX + side * 16 + index
            part = pair_ref[base : base + 1, :]
            value = part if value is None else value + part
    return value


def position():
    return lax.axis_index("gz"), lax.axis_size("gz"), lax.axis_index("xy"), lax.axis_size("xy")


def edge_kernel(pair_ref, edge_ref):
    at_z, _, at_x, _ = position()
    to_right = ((at_z + at_x) & 1) == 0
    for n in range(CHIP_ROWS):
        value = chip_row(pair_ref, n - 1)
        edge_ref[n * 8 : (n + 1) * 8, :] = jnp.where(to_right, value[8:], value[:8])
        left, right = (chip_margin(pair_ref, side, n - 1) for side in range(2))
        edge_ref[CHIP_ROWS * 8 + n : CHIP_ROWS * 8 + n + 1, :] = jnp.where(to_right, right, left)
    edge_ref[CHIP_ROWS * 9 :, :] = jnp.zeros((EDGE - CHIP_ROWS * 9, YC), jnp.float32)


def chip_kernel(pair_ref, edges_ref, chip_ref, send_ref):
    at_z, _, at_x, count_x = position()
    odd_x = at_x & 1
    from_left = (1 - odd_x) * (2 * EDGE)
    from_right = odd_x * (2 * EDGE) + EDGE
    sub = iota((8, YC), 0)
    has_left = jnp.where(at_x > 0, 1.0, 0.0)
    has_right = jnp.where(at_x < count_x - 1, 1.0, 0.0)
    upper_core = (at_z & 1) == 1

    def part(start, offset, count):
        return edges_ref[pl.ds(pl.multiple_of(start, 8) + offset, count), :]

    left_margins = [part(from_left, CHIP_ROWS * 8 + 8 * n, 8) * has_left for n in range(3)]
    right_margins = [part(from_right, CHIP_ROWS * 8 + 8 * n, 8) * has_right for n in range(3)]
    for n in range(CHIP_ROWS):
        own = chip_row(pair_ref, n - 1)
        first_margin, last_margin = (chip_margin(pair_ref, side, n - 1) for side in range(2))
        block, at = divmod(n, 8)
        left_margin = left_margins[block][at : at + 1]
        right_margin = right_margins[block][at : at + 1]
        sums = (
            part(from_left, n * 8, 8) * has_left + jnp.where(sub == 7, first_margin, 0.0),
            own[:8] + jnp.where(sub == 0, left_margin, 0.0),
            own[8:] + jnp.where(sub == 7, right_margin, 0.0),
            part(from_right, n * 8, 8) * has_right + jnp.where(sub == 0, last_margin, 0.0),
        )
        for k in range(4):
            at = n * 32 + k * 8
            chip_ref[at : at + 8, :] = sums[k]
            low = k * 8 + n * 32
            high = k * 8 + (n - SEND_ROWS) * 32
            if n < SEND_ROWS:

                @pl.when(jnp.logical_not(upper_core))
                def _(value=sums[k], low=low):
                    send_ref[low : low + 8, :] = value

            else:

                @pl.when(upper_core)
                def _(value=sums[k], high=high):
                    send_ref[high : high + 8, :] = value


def two_terms(values):
    upper = values.astype(jnp.bfloat16)
    lower = (values - upper.astype(jnp.float32)).astype(jnp.bfloat16)
    return upper, lower


def vessel_kernel(
    chip_ref,
    slabs_ref,
    rows_ref,
    tissue_ref,
    x_ref,
    y_ref,
    probability_ref,
    vessel_ref,
    extended_ref,
    along_z_ref,
):
    at_z, count_z, at_x, count_x = position()
    upper_core = (at_z & 1) == 1
    below = jnp.where(at_z - (at_z & 1) > 0, 1.0, 0.0)
    above = jnp.where(at_z - (at_z & 1) < count_z - 2, 1.0, 0.0)

    @pl.when(jnp.logical_not(upper_core))
    def _():
        for z in range(3 * CZ):
            value = None
            if z >= RIM - 1:
                n = z - RIM + 1
                value = chip_ref[n * 32 : (n + 1) * 32, :]
            if z < SEND_ROWS:
                part = slabs_ref[z * 32 : (z + 1) * 32, :] * below
                value = part if value is None else value + part
            if z == 3 * CZ - 1:
                value = value + rows_ref[96:128, :] * above
            extended_ref[z * 32 : (z + 1) * 32, :] = value

    @pl.when(upper_core)
    def _():
        for z in range(3 * CZ):
            value = None
            if z + 1 < CHIP_ROWS:
                value = chip_ref[(z + 1) * 32 : (z + 2) * 32, :]
            if z >= 3 * CZ - SEND_ROWS:
                n = SEND_ROWS + z - (3 * CZ - SEND_ROWS)
                part = slabs_ref[n * 32 : (n + 1) * 32, :] * above
                value = part if value is None else value + part
            if z == 0:
                value = value + rows_ref[0:32, :] * below
            extended_ref[z * 32 : (z + 1) * 32, :] = value

    sub = iota((8, YC), 0)

    def inverse_x(first, edge, edge_row, present):
        cover = jnp.zeros((8, YC), jnp.float32)
        for j in range(8):
            cover = jnp.where(sub == j, float(WINDOW_X[first + j + 1]), cover)
        extra = jnp.where(present, float(edge), 0.0)
        return 1.0 / (cover + jnp.where(sub == edge_row, extra, 0.0))

    wx_last, wx_first = WINDOW_X[SPAN_X - 1], WINDOW_X[0]
    yes = at_x >= 0
    inverse = [
        inverse_x(8, wx_first, 7, yes),
        inverse_x(0, wx_last, 0, at_x > 0),
        inverse_x(8, wx_first, 7, at_x < count_x - 1),
        inverse_x(0, wx_last, 0, yes),
    ]
    wz_last, wz_first = WINDOW_Z[SPAN_Z - 1], WINDOW_Z[0]
    lower_there = (at_z > 1, at_z > 0, yes)
    upper_there = (yes, at_z < count_z - 1, at_z < count_z - 2)
    inside_x = (at_x > 0, yes, yes, at_x < count_x - 1)
    inside_z = (at_z > 0, yes, at_z < count_z - 1)
    keep_x = [jnp.where(flag, 1.0, 0.0) for flag in inside_x]
    keep_z = [jnp.where(flag, 1.0, 0.0) for flag in inside_z]
    for z in range(3 * CZ):
        block, i = divmod(z, CZ)
        plain = WINDOW_Z[i + 1]
        scale = float(1.0 / plain)
        if i == 0:
            scale = jnp.where(lower_there[block], float(1.0 / (plain + wz_last)), scale)
        if i == CZ - 1:
            scale = jnp.where(upper_there[block], float(1.0 / (plain + wz_first)), scale)
        for k in range(4):
            blended = extended_ref[z * 32 + k * 8 : z * 32 + k * 8 + 8, :]
            value = 1.0 / (1.0 + jnp.exp(-(blended * (inverse[k] * scale))))
            if block == 1 and k in (1, 2):
                at = i * CX + (k - 1) * 8
                probability_ref[at : at + 8, :] = value
            else:
                value = value * (keep_x[k] * keep_z[block])
            extended_ref[z * 32 + k * 8 : z * 32 + k * 8 + 8, :] = value

    weights = [[taps(radius, degree) for degree in range(3)] for radius in RADII]

    def filter_z(n, radius):
        for i in range(CZ):

            def plane(offset):
                at = (i + RIM + offset) * 32
                return extended_ref[at : at + 32, :]

            centre = plane(0)
            results = [centre * float(weights[n][degree][radius]) for degree in range(3)]
            for k in range(1, radius + 1):
                before, after = plane(-k), plane(k)
                both, change = before + after, before - after
                for degree in range(3):
                    term = (change if degree == 1 else both) * float(weights[n][degree][radius + k])
                    fresh = degree == 1 and k == 1
                    results[degree] = term if fresh else results[degree] + term
            for degree in range(3):
                upper, lower = two_terms(results[degree])
                base = (n * 3 + degree) * 96
                for at, part in ((0, upper), (32, lower), (64, upper)):
                    along_z_ref[base + at : base + at + 32, i * YC : (i + 1) * YC] = part

    total = jnp.zeros((CZ * CX, YC), jnp.float32)
    filter_z(0, RADII[0])
    for n in range(3):
        if n < 2:
            filter_z(n + 1, RADII[n + 1])
        after_x = {}
        for degree in range(3):
            data = along_z_ref[(n * 3 + degree) * 96 : (n * 3 + degree + 1) * 96, :]
            wide = jnp.dot(
                x_ref[n, : (3 - degree) * CX], data, preferred_element_type=jnp.float32
            )
            for other in range(3 - degree):
                rows = wide[other * CX : (other + 1) * CX]
                after_x[degree, other] = jnp.concatenate(
                    [rows[:, z * YC : (z + 1) * YC] for z in range(CZ)], axis=0
                )

        def along_y(degree, keys):
            stacked = jnp.concatenate([after_x[key] for key in keys], axis=0)
            pair = jnp.concatenate(two_terms(stacked), axis=1)
            wide = jnp.dot(pair, y_ref[n * 3 + degree], preferred_element_type=jnp.float32)
            summed = wide[:, :YC] + wide[:, YC:]
            return [summed[at * 128 : (at + 1) * 128] for at in range(len(keys))]

        hzz, hxx, hzx = along_y(0, ((2, 0), (0, 2), (1, 1)))
        hzy, hxy = along_y(1, ((1, 0), (0, 1)))
        (hyy,) = along_y(2, ((0, 0),))
        first_inv = hzz + hxx + hyy
        second_inv = hzz * hxx + hzz * hyy + hxx * hyy - hzx * hzx - hzy * hzy - hxy * hxy
        third_inv = (
            hzz * (hxx * hyy - hxy * hxy)
            - hzx * (hzx * hyy - hxy * hzy)
            + hzy * (hzx * hxy - hxx * hzy)
        )
        positive = jnp.maximum(second_inv, 0.0)
        size = jnp.abs(third_inv)
        root = jnp.where(size > 0.0, jnp.exp(jnp.log(size) * (2.0 / 3.0)), 0.0)
        total = total + jnp.maximum(-first_inv, 0.0) * positive / (positive + root + TUBE_FLOOR)
    vessel_ref[...] = VESSEL_GAIN * tissue_ref[...].astype(jnp.float32) * total


def pairs_of(kind, count_z, count_x):
    def flat(z, x):
        return (z % count_z) * count_x + x % count_x

    if kind == "chip":
        return [
            [flat(z, x), flat(z + 1, x)] for z in range(0, count_z, 2) for x in range(count_x)
        ]
    if kind == "slab":
        pairs = [
            [flat(z, x), flat(z + 1, x)] for z in range(1, count_z - 1, 2) for x in range(count_x)
        ]
        return pairs + [
            [flat(z, x), flat(z, x + 1)] for z in (0, count_z - 1) for x in range(0, count_x, 2)
        ]
    pairs = [
        [flat(z, x), flat(z, x + 1)] for z in range(count_z) for x in range(z % 2, count_x - 1, 2)
    ]
    if count_z % 8 == 0:
        idle = [(z, z + 4) for z in range(1, count_z, 2) if z % 8 < 4]
        return pairs + [[flat(z, x), flat(up, x)] for z, up in idle for x in (0, count_x - 1)]
    return pairs + [[flat(z, count_x - 1), flat(z, 0)] for z in range(1, count_z, 2)]


def swap(block, kind):
    groups = pairs_of(kind, lax.axis_size("gz"), lax.axis_size("xy"))
    return lax.all_gather(block, ("gz", "xy"), axis_index_groups=groups, tiled=True)


def whole(count, space=pltpu.VMEM):
    return [pl.BlockSpec(memory_space=space)] * count


def shape_of(*dims):
    return jax.ShapeDtypeStruct(dims, jnp.float32)


def decode(patch_features, conv1_weight, conv1_bias, conv2_weight, conv2_bias, head_weight):
    f32, bf16 = jnp.float32, jnp.bfloat16
    weight_shape = (3, 3, 3, CHANNELS, CHANNELS)
    slots = ((HALF + 2) * SLOT, 2 * YC)
    return pl.pallas_call(
        decoder_kernel,
        out_shape=shape_of(PATCH, YC),
        in_specs=whole(6, pltpu.HBM),
        out_specs=whole(1)[0],
        scratch_shapes=[
            pltpu.VMEM((SPAN_Z, SPAN_X, CHANNELS, YC), bf16),
            pltpu.VMEM(weight_shape, bf16),
            pltpu.VMEM((1, CHANNELS), f32),
            pltpu.VMEM(weight_shape, bf16),
            pltpu.VMEM((1, CHANNELS), f32),
            pltpu.VMEM((1, CHANNELS), bf16),
            pltpu.VMEM(slots, bf16),
            pltpu.VMEM(slots, bf16),
            pltpu.VMEM((9 * CHANNELS, 3 * REACH), bf16),
            pltpu.VMEM((9 * CHANNELS, 3 * REACH), bf16),
            pltpu.VMEM((ROWS, SPAN_X * YC), bf16),
            pltpu.SemaphoreType.DMA((6,)),
        ],
        compiler_params=pltpu.CompilerParams(vmem_limit_bytes=DECODER_VMEM_LIMIT),
        name="decoder",
    )(
        patch_features.transpose(1, 2, 0, 3),
        conv1_weight.transpose(2, 3, 4, 0, 1),
        conv1_bias.reshape(1, CHANNELS),
        conv2_weight.transpose(2, 3, 4, 0, 1),
        conv2_bias.reshape(1, CHANNELS),
        head_weight.reshape(1, CHANNELS),
    )


def measure_tubes(chip, slabs, rows, tissue_mask):
    f32, bf16 = jnp.float32, jnp.bfloat16
    params = pltpu.CompilerParams(vmem_limit_bytes=VMEM_LIMIT)
    x_all, y_all = filter_constants()
    return pl.pallas_call(
        vessel_kernel,
        out_shape=(shape_of(CZ * CX, YC), shape_of(CZ * CX, YC)),
        in_specs=whole(6),
        out_specs=tuple(whole(2)),
        scratch_shapes=[
            pltpu.VMEM((3 * CZ * 32, YC), f32),
            pltpu.VMEM((9 * 96, CZ * YC), bf16),
        ],
        compiler_params=params,
        name="vessel",
    )(
        chip,
        slabs,
        rows,
        tissue_mask.reshape(CZ * CX, YC),
        jnp.asarray(x_all),
        jnp.asarray(y_all),
    )


def on_device(
    patch_features, conv1_weight, conv1_bias, conv2_weight, conv2_bias, head_weight, tissue_mask
):
    params = pltpu.CompilerParams(vmem_limit_bytes=VMEM_LIMIT)
    patch = decode(
        patch_features, conv1_weight, conv1_bias, conv2_weight, conv2_bias, head_weight
    )
    pair = swap(patch, "chip")
    edge = pl.pallas_call(
        edge_kernel,
        out_shape=shape_of(EDGE, YC),
        in_specs=whole(1),
        out_specs=whole(1)[0],
        compiler_params=params,
        name="edge",
    )(pair)
    edges = swap(swap(edge, "x"), "chip")
    chip, send = pl.pallas_call(
        chip_kernel,
        out_shape=(shape_of(CHIP_ROWS * 32, YC), shape_of(SEND_ROWS * 32, YC)),
        in_specs=whole(2),
        out_specs=tuple(whole(2)),
        compiler_params=params,
        name="chip",
    )(pair, edges)
    slabs = swap(send, "slab")
    near = (SEND_ROWS - 1) * 32
    rows = swap(slabs[near : near + 64], "chip")
    probability, vesselness = measure_tubes(chip, slabs, rows, tissue_mask)
    return (
        probability.reshape(CZ, CX, YC),
        vesselness.reshape(CZ, CX, YC),
    )


def solution(mesh):
    placed = (P(None, "gz", "xy", None), P(), P(), P(), P(), P(), P("gz", "xy", None))
    return jax.shard_map(
        on_device,
        mesh=mesh,
        in_specs=placed,
        out_specs=(P("gz", "xy", None), P("gz", "xy", None)),
        check_vma=False,
    )
```

```python
import jax
import jax.numpy as jnp
import numpy as np
from jax import lax
from jax.experimental import pallas as pl
from jax.experimental.pallas import tpu as pltpu
from jax.sharding import PartitionSpec as P

CHANNELS = 16
CZ = 8
CX = 16
YC = 128
MARGIN = 1
RIM = 8
SPAN_Z = CZ + 2 * MARGIN
SPAN_X = CX + 2 * MARGIN
HALF = SPAN_X // 2
ROWS = SPAN_Z * CHANNELS
SLOT = ROWS + 3 * CHANNELS
REACH = 5 * CHANNELS
BLOCKS = ((0, 3), (3, 3), (6, 2), (8, 2))
RADII = (RIM // 4, RIM // 2, RIM)
VESSEL_GAIN = 4.0
TUBE_FLOOR = 0.01
PATCH = SPAN_Z * CX + 2 * 16
CHIP_ROWS = 2 * CZ + 2
EDGE = 168
SEND_ROWS = CHIP_ROWS // 2
VMEM_LIMIT = 24 * 1024 * 1024
DECODER_VMEM_LIMIT = 63 * 1024 * 1024


def window(size):
    position = np.arange(size, dtype=np.float64)
    return np.exp(-0.5 * ((position - (size - 1) / 2.0) / (size / 4.0)) ** 2)


WINDOW_Z = window(SPAN_Z)
WINDOW_X = window(SPAN_X)


def taps(radius, degree):
    spread = radius / 3.0
    offsets = np.arange(-radius, radius + 1, dtype=np.float64)
    gaussian = np.exp(-offsets * offsets / (2.0 * spread * spread))
    gaussian = gaussian / gaussian.sum()
    if degree == 1:
        return -offsets / spread**2 * gaussian
    if degree == 2:
        return (offsets**2 / spread**4 - 1.0 / spread**2) * gaussian
    return gaussian


def band(out_len, in_len, offset, radius, degree):
    weights = taps(radius, degree)
    distance = np.arange(out_len)[:, None] + offset - np.arange(in_len)[None, :]
    inside = np.abs(distance) <= radius
    return np.where(inside, weights[np.clip(distance, -radius, radius) + radius], 0.0)


def split_terms(matrix):
    whole = matrix.astype(np.float32)
    upper = whole.astype(jnp.bfloat16)
    lower = (whole - upper.astype(np.float32)).astype(jnp.bfloat16)
    return upper, lower


def filter_constants():
    x_all, y_all = [], []
    for radius in RADII:
        blocks = [band(CX, CX + 2 * RIM, RIM, radius, degree) for degree in range(3)]
        upper, lower = split_terms(np.concatenate(blocks, axis=0))
        x_all.append(np.concatenate([upper, upper, lower], axis=1))
        for degree in range(3):
            scaled = (radius / 3.0) ** 2 * band(YC, YC, 0, radius, degree).T
            upper, lower = split_terms(scaled)
            top = np.concatenate([upper, lower], axis=1)
            bottom = np.concatenate([upper, np.zeros_like(lower)], axis=1)
            y_all.append(np.concatenate([top, bottom], axis=0))
    return np.stack(x_all), np.stack(y_all)


def iota(shape, dim):
    return lax.broadcasted_iota(jnp.int32, shape, dim)


def sum_over_y(parts):
    lane = iota(parts[0].shape, 1)
    before = jnp.where(lane == 0, 0.0, pltpu.roll(parts[0], 1, 1))
    after = jnp.where(lane == YC - 1, 0.0, pltpu.roll(parts[2], YC - 1, 1))
    return before + parts[1] + after


def store_part(slots_ref, slot, half, z, part):
    at = slot * SLOT + (z + 1) * CHANNELS
    slots_ref[at : at + part.shape[0], half * YC : (half + 1) * YC] = part


def expand_weight(weight_ref, wide_ref):
    shape = (CHANNELS, 3 * REACH)
    lane = iota(shape, 1)
    group = (lane >= REACH).astype(jnp.int32) + (lane >= 2 * REACH).astype(jnp.int32)
    same = (lane & (CHANNELS - 1)) == iota(shape, 0)
    spread = jnp.zeros((9 * CHANNELS, 3 * REACH), jnp.float32)
    for dx in range(3):
        pick = jnp.where(same & (group == dx), 1.0, 0.0).astype(jnp.bfloat16)
        part = weight_ref[:, dx].reshape(9 * CHANNELS, CHANNELS)
        spread = spread + jnp.dot(part, pick, preferred_element_type=jnp.float32)
    plane = (lane - group * REACH) >> 4
    for z in range(3):
        for dy in range(3):
            rows = jnp.zeros(shape, jnp.float32)
            for dz in range(3):
                at = (dz * 3 + dy) * CHANNELS
                rows = jnp.where(plane == z + dz, spread[at : at + CHANNELS], rows)
            at = (z * 3 + dy) * CHANNELS
            wide_ref[at : at + CHANNELS, :] = rows.astype(jnp.bfloat16)


def column_of(row_ref):
    eye = iota((CHANNELS, CHANNELS), 0) == iota((CHANNELS, CHANNELS), 1)
    row = row_ref[...].astype(jnp.float32)
    return jnp.sum(jnp.where(eye, row, 0.0), axis=1, keepdims=True)


def decoder_kernel(
    features_hbm,
    weight1_hbm,
    bias1_hbm,
    weight2_hbm,
    bias2_hbm,
    head_hbm,
    patch_ref,
    features_ref,
    weight1_ref,
    bias1_ref,
    weight2_ref,
    bias2_ref,
    head_ref,
    first_ref,
    second_ref,
    wide1_ref,
    wide2_ref,
    arrived,
):
    routes = (
        (weight1_hbm, weight1_ref),
        (weight2_hbm, weight2_ref),
        (bias1_hbm, bias1_ref),
        (bias2_hbm, bias2_ref),
        (head_hbm, head_ref),
        (features_hbm, features_ref),
    )
    copies = [
        pltpu.make_async_copy(source, target, arrived.at[k])
        for k, (source, target) in enumerate(routes)
    ]
    for copy in copies:
        copy.start()
    for ref in (first_ref, second_ref):
        ref[0:SLOT, 0:YC] = jnp.zeros((SLOT, YC), jnp.bfloat16)
        ref[(HALF + 1) * SLOT :, YC:] = jnp.zeros((SLOT, YC), jnp.bfloat16)
        for slot in range(HALF + 2):
            base = slot * SLOT
            ref[base : base + CHANNELS, :] = jnp.zeros((CHANNELS, 2 * YC), jnp.bfloat16)
            ref[base + CHANNELS + ROWS : base + SLOT, :] = jnp.zeros(
                (2 * CHANNELS, 2 * YC), jnp.bfloat16
            )
    copies[0].wait()
    expand_weight(weight1_ref, wide1_ref)
    copies[1].wait()
    expand_weight(weight2_ref, wide2_ref)
    for copy in copies[2:]:
        copy.wait()
    for x in range(SPAN_X):
        column = features_ref[:, x].reshape(ROWS, YC)
        if x <= HALF:
            store_part(first_ref, x + 1, 0, 0, column)
        if x >= HALF - 1:
            store_part(first_ref, x - HALF + 1, 1, 0, column)

    def layer(wide_ref, slots_ref, bias, step, put):
        for first, count in BLOCKS:
            pieces = []
            for dx in range(3):
                at = (step + dx) * SLOT + first * CHANNELS
                pieces.append(slots_ref[at : at + REACH, :])
            summed = jnp.dot(
                wide_ref[: count * 3 * CHANNELS],
                jnp.concatenate(pieces, axis=0),
                preferred_element_type=jnp.float32,
            )
            for z in range(count):
                for half in range(2):
                    parts = []
                    for dy in range(3):
                        at = (z * 3 + dy) * CHANNELS
                        parts.append(summed[at : at + CHANNELS, half * YC : (half + 1) * YC])
                    value = jnp.maximum(sum_over_y(parts) + bias, 0.0)
                    put(first + z, half, value.astype(jnp.bfloat16))

    bias1 = column_of(bias1_ref)
    for step in range(HALF):

        def put_first(z, half, part, step=step):
            store_part(second_ref, step + 1, half, z, part)
            if half == 0 and step == HALF - 1:
                store_part(second_ref, 0, 1, z, part)
            if half == 1 and step == 0:
                store_part(second_ref, HALF + 1, 0, z, part)

        layer(wide1_ref, first_ref, bias1, step, put_first)

    bias2 = column_of(bias2_ref)
    head_column = column_of(head_ref)
    patch_ref[SPAN_Z * CX :, :] = jnp.zeros((PATCH - SPAN_Z * CX, YC), jnp.float32)
    for step in range(HALF):

        def put_last(z, half, part, step=step):
            x = step + half * HALF
            scaled = part.astype(jnp.float32) * head_column
            logit = jnp.sum(scaled, axis=0, keepdims=True)
            weighted = logit * float(WINDOW_Z[z] * WINDOW_X[x])
            at = z * CX + x - 1
            if x == 0:
                at = SPAN_Z * CX + z
            elif x == SPAN_X - 1:
                at = SPAN_Z * CX + 16 + z
            patch_ref[at : at + 1, :] = weighted

        layer(wide2_ref, second_ref, bias2, step, put_last)


def chip_row(pair_ref, r):
    low, high = r + 1, r - CZ + 1
    value = None
    for patch, index in ((0, low), (1, high)):
        if 0 <= index < SPAN_Z:
            base = patch * PATCH + index * CX
            part = pair_ref[base : base + CX, :]
            value = part if value is None else value + part
    return value


def chip_margin(pair_ref, side, r):
    low, high = r + 1, r - CZ + 1
    value = None
    for patch, index in ((0, low), (1, high)):
        if 0 <= index < SPAN_Z:
            base = patch * PATCH + SPAN_Z * CX + side * 16 + index
            part = pair_ref[base : base + 1, :]
            value = part if value is None else value + part
    return value


def position():
    return lax.axis_index("gz"), lax.axis_size("gz"), lax.axis_index("xy"), lax.axis_size("xy")


def edge_kernel(pair_ref, edge_ref):
    at_z, _, at_x, _ = position()
    to_right = ((at_z + at_x) & 1) == 0
    for n in range(CHIP_ROWS):
        value = chip_row(pair_ref, n - 1)
        edge_ref[n * 8 : (n + 1) * 8, :] = jnp.where(to_right, value[8:], value[:8])
        left, right = (chip_margin(pair_ref, side, n - 1) for side in range(2))
        edge_ref[CHIP_ROWS * 8 + n : CHIP_ROWS * 8 + n + 1, :] = jnp.where(to_right, right, left)
    edge_ref[CHIP_ROWS * 9 :, :] = jnp.zeros((EDGE - CHIP_ROWS * 9, YC), jnp.float32)


def chip_kernel(pair_ref, edges_ref, chip_ref, send_ref):
    at_z, _, at_x, count_x = position()
    odd_x = at_x & 1
    from_left = (1 - odd_x) * (2 * EDGE)
    from_right = odd_x * (2 * EDGE) + EDGE
    sub = iota((8, YC), 0)
    has_left = jnp.where(at_x > 0, 1.0, 0.0)
    has_right = jnp.where(at_x < count_x - 1, 1.0, 0.0)
    upper_core = (at_z & 1) == 1

    def part(start, offset, count):
        return edges_ref[pl.ds(pl.multiple_of(start, 8) + offset, count), :]

    left_margins = [part(from_left, CHIP_ROWS * 8 + 8 * n, 8) * has_left for n in range(3)]
    right_margins = [part(from_right, CHIP_ROWS * 8 + 8 * n, 8) * has_right for n in range(3)]
    for n in range(CHIP_ROWS):
        own = chip_row(pair_ref, n - 1)
        first_margin, last_margin = (chip_margin(pair_ref, side, n - 1) for side in range(2))
        block, at = divmod(n, 8)
        left_margin = left_margins[block][at : at + 1]
        right_margin = right_margins[block][at : at + 1]
        sums = (
            part(from_left, n * 8, 8) * has_left + jnp.where(sub == 7, first_margin, 0.0),
            own[:8] + jnp.where(sub == 0, left_margin, 0.0),
            own[8:] + jnp.where(sub == 7, right_margin, 0.0),
            part(from_right, n * 8, 8) * has_right + jnp.where(sub == 0, last_margin, 0.0),
        )
        for k in range(4):
            at = n * 32 + k * 8
            chip_ref[at : at + 8, :] = sums[k]
            low = k * 8 + n * 32
            high = k * 8 + (n - SEND_ROWS) * 32
            if n < SEND_ROWS:

                @pl.when(jnp.logical_not(upper_core))
                def _(value=sums[k], low=low):
                    send_ref[low : low + 8, :] = value

            else:

                @pl.when(upper_core)
                def _(value=sums[k], high=high):
                    send_ref[high : high + 8, :] = value


def two_terms(values):
    upper = values.astype(jnp.bfloat16)
    lower = (values - upper.astype(jnp.float32)).astype(jnp.bfloat16)
    return upper, lower


def vessel_kernel(
    chip_ref,
    slabs_ref,
    rows_ref,
    tissue_ref,
    x_ref,
    y_ref,
    probability_ref,
    vessel_ref,
    extended_ref,
    along_z_ref,
):
    at_z, count_z, at_x, count_x = position()
    upper_core = (at_z & 1) == 1
    below = jnp.where(at_z - (at_z & 1) > 0, 1.0, 0.0)
    above = jnp.where(at_z - (at_z & 1) < count_z - 2, 1.0, 0.0)

    @pl.when(jnp.logical_not(upper_core))
    def _():
        for z in range(3 * CZ):
            value = None
            if z >= RIM - 1:
                n = z - RIM + 1
                value = chip_ref[n * 32 : (n + 1) * 32, :]
            if z < SEND_ROWS:
                part = slabs_ref[z * 32 : (z + 1) * 32, :] * below
                value = part if value is None else value + part
            if z == 3 * CZ - 1:
                value = value + rows_ref[32:64, :] * above
            extended_ref[z * 32 : (z + 1) * 32, :] = value

    @pl.when(upper_core)
    def _():
        for z in range(3 * CZ):
            value = None
            if z + 1 < CHIP_ROWS:
                value = chip_ref[(z + 1) * 32 : (z + 2) * 32, :]
            if z >= 3 * CZ - SEND_ROWS:
                n = SEND_ROWS + z - (3 * CZ - SEND_ROWS)
                part = slabs_ref[n * 32 : (n + 1) * 32, :] * above
                value = part if value is None else value + part
            if z == 0:
                value = value + rows_ref[0:32, :] * below
            extended_ref[z * 32 : (z + 1) * 32, :] = value

    sub = iota((8, YC), 0)

    def inverse_x(first, edge, edge_row, present):
        cover = jnp.zeros((8, YC), jnp.float32)
        for j in range(8):
            cover = jnp.where(sub == j, float(WINDOW_X[first + j + 1]), cover)
        extra = jnp.where(present, float(edge), 0.0)
        return 1.0 / (cover + jnp.where(sub == edge_row, extra, 0.0))

    wx_last, wx_first = WINDOW_X[SPAN_X - 1], WINDOW_X[0]
    yes = at_x >= 0
    inverse = [
        inverse_x(8, wx_first, 7, yes),
        inverse_x(0, wx_last, 0, at_x > 0),
        inverse_x(8, wx_first, 7, at_x < count_x - 1),
        inverse_x(0, wx_last, 0, yes),
    ]
    wz_last, wz_first = WINDOW_Z[SPAN_Z - 1], WINDOW_Z[0]
    lower_there = (at_z > 1, at_z > 0, yes)
    upper_there = (yes, at_z < count_z - 1, at_z < count_z - 2)
    inside_x = (at_x > 0, yes, yes, at_x < count_x - 1)
    inside_z = (at_z > 0, yes, at_z < count_z - 1)
    keep_x = [jnp.where(flag, 1.0, 0.0) for flag in inside_x]
    keep_z = [jnp.where(flag, 1.0, 0.0) for flag in inside_z]
    for z in range(3 * CZ):
        block, i = divmod(z, CZ)
        plain = WINDOW_Z[i + 1]
        scale = float(1.0 / plain)
        if i == 0:
            scale = jnp.where(lower_there[block], float(1.0 / (plain + wz_last)), scale)
        if i == CZ - 1:
            scale = jnp.where(upper_there[block], float(1.0 / (plain + wz_first)), scale)
        for k in range(4):
            blended = extended_ref[z * 32 + k * 8 : z * 32 + k * 8 + 8, :]
            value = 1.0 / (1.0 + jnp.exp(-(blended * (inverse[k] * scale))))
            if block == 1 and k in (1, 2):
                at = i * CX + (k - 1) * 8
                probability_ref[at : at + 8, :] = value
            else:
                value = value * (keep_x[k] * keep_z[block])
            extended_ref[z * 32 + k * 8 : z * 32 + k * 8 + 8, :] = value

    weights = [[taps(radius, degree) for degree in range(3)] for radius in RADII]

    def filter_z(n, radius):
        for i in range(CZ):

            def plane(offset):
                at = (i + RIM + offset) * 32
                return extended_ref[at : at + 32, :]

            centre = plane(0)
            results = [centre * float(weights[n][degree][radius]) for degree in range(3)]
            for k in range(1, radius + 1):
                before, after = plane(-k), plane(k)
                both, change = before + after, before - after
                for degree in range(3):
                    term = (change if degree == 1 else both) * float(weights[n][degree][radius + k])
                    fresh = degree == 1 and k == 1
                    results[degree] = term if fresh else results[degree] + term
            for degree in range(3):
                upper, lower = two_terms(results[degree])
                base = (n * 3 + degree) * 96
                for at, part in ((0, upper), (32, lower), (64, upper)):
                    along_z_ref[base + at : base + at + 32, i * YC : (i + 1) * YC] = part

    total = jnp.zeros((CZ * CX, YC), jnp.float32)
    filter_z(0, RADII[0])
    for n in range(3):
        if n < 2:
            filter_z(n + 1, RADII[n + 1])
        after_x = {}
        for degree in range(3):
            data = along_z_ref[(n * 3 + degree) * 96 : (n * 3 + degree + 1) * 96, :]
            wide = jnp.dot(
                x_ref[n, : (3 - degree) * CX], data, preferred_element_type=jnp.float32
            )
            for other in range(3 - degree):
                rows = wide[other * CX : (other + 1) * CX]
                after_x[degree, other] = jnp.concatenate(
                    [rows[:, z * YC : (z + 1) * YC] for z in range(CZ)], axis=0
                )

        def along_y(degree, keys):
            stacked = jnp.concatenate([after_x[key] for key in keys], axis=0)
            pair = jnp.concatenate(two_terms(stacked), axis=1)
            wide = jnp.dot(pair, y_ref[n * 3 + degree], preferred_element_type=jnp.float32)
            summed = wide[:, :YC] + wide[:, YC:]
            return [summed[at * 128 : (at + 1) * 128] for at in range(len(keys))]

        hzz, hxx, hzx = along_y(0, ((2, 0), (0, 2), (1, 1)))
        hzy, hxy = along_y(1, ((1, 0), (0, 1)))
        (hyy,) = along_y(2, ((0, 0),))
        first_inv = hzz + hxx + hyy
        second_inv = hzz * hxx + hzz * hyy + hxx * hyy - hzx * hzx - hzy * hzy - hxy * hxy
        third_inv = (
            hzz * (hxx * hyy - hxy * hxy)
            - hzx * (hzx * hyy - hxy * hzy)
            + hzy * (hzx * hxy - hxx * hzy)
        )
        positive = jnp.maximum(second_inv, 0.0)
        size = jnp.abs(third_inv)
        root = jnp.where(size > 0.0, jnp.exp(jnp.log(size) * (2.0 / 3.0)), 0.0)
        total = total + jnp.maximum(-first_inv, 0.0) * positive / (positive + root + TUBE_FLOOR)
    vessel_ref[...] = VESSEL_GAIN * tissue_ref[...].astype(jnp.float32) * total


def pairs_of(kind, count_z, count_x):
    def flat(z, x):
        return (z % count_z) * count_x + x % count_x

    if kind == "chip":
        return [
            [flat(z, x), flat(z + 1, x)] for z in range(0, count_z, 2) for x in range(count_x)
        ]
    if kind == "slab":
        pairs = [
            [flat(z, x), flat(z + 1, x)] for z in range(1, count_z - 1, 2) for x in range(count_x)
        ]
        return pairs + [
            [flat(z, x), flat(z, x + 1)] for z in (0, count_z - 1) for x in range(0, count_x, 2)
        ]
    pairs = [
        [flat(z, x), flat(z, x + 1)] for z in range(count_z) for x in range(z % 2, count_x - 1, 2)
    ]
    if count_z % 8 == 0:
        idle = [(z, z + 4) for z in range(1, count_z, 2) if z % 8 < 4]
        return pairs + [[flat(z, x), flat(up, x)] for z, up in idle for x in (0, count_x - 1)]
    return pairs + [[flat(z, count_x - 1), flat(z, 0)] for z in range(1, count_z, 2)]


def swap(block, kind):
    groups = pairs_of(kind, lax.axis_size("gz"), lax.axis_size("xy"))
    return lax.all_gather(block, ("gz", "xy"), axis_index_groups=groups, tiled=True)


def whole(count, space=pltpu.VMEM):
    return [pl.BlockSpec(memory_space=space)] * count


def shape_of(*dims):
    return jax.ShapeDtypeStruct(dims, jnp.float32)


def decode(patch_features, conv1_weight, conv1_bias, conv2_weight, conv2_bias, head_weight):
    f32, bf16 = jnp.float32, jnp.bfloat16
    weight_shape = (3, 3, 3, CHANNELS, CHANNELS)
    slots = ((HALF + 2) * SLOT, 2 * YC)
    return pl.pallas_call(
        decoder_kernel,
        out_shape=shape_of(PATCH, YC),
        in_specs=whole(6, pltpu.HBM),
        out_specs=whole(1)[0],
        scratch_shapes=[
            pltpu.VMEM((SPAN_Z, SPAN_X, CHANNELS, YC), bf16),
            pltpu.VMEM(weight_shape, bf16),
            pltpu.VMEM((1, CHANNELS), f32),
            pltpu.VMEM(weight_shape, bf16),
            pltpu.VMEM((1, CHANNELS), f32),
            pltpu.VMEM((1, CHANNELS), bf16),
            pltpu.VMEM(slots, bf16),
            pltpu.VMEM(slots, bf16),
            pltpu.VMEM((9 * CHANNELS, 3 * REACH), bf16),
            pltpu.VMEM((9 * CHANNELS, 3 * REACH), bf16),
            pltpu.SemaphoreType.DMA((6,)),
        ],
        compiler_params=pltpu.CompilerParams(vmem_limit_bytes=DECODER_VMEM_LIMIT),
        name="decoder",
    )(
        patch_features.transpose(1, 2, 0, 3),
        conv1_weight.transpose(2, 3, 4, 0, 1),
        conv1_bias.reshape(1, CHANNELS),
        conv2_weight.transpose(2, 3, 4, 0, 1),
        conv2_bias.reshape(1, CHANNELS),
        head_weight.reshape(1, CHANNELS),
    )


def measure_tubes(chip, slabs, rows, tissue_mask):
    f32, bf16 = jnp.float32, jnp.bfloat16
    params = pltpu.CompilerParams(vmem_limit_bytes=VMEM_LIMIT)
    x_all, y_all = filter_constants()
    return pl.pallas_call(
        vessel_kernel,
        out_shape=(shape_of(CZ * CX, YC), shape_of(CZ * CX, YC)),
        in_specs=whole(6),
        out_specs=tuple(whole(2)),
        scratch_shapes=[
            pltpu.VMEM((3 * CZ * 32, YC), f32),
            pltpu.VMEM((9 * 96, CZ * YC), bf16),
        ],
        compiler_params=params,
        name="vessel",
    )(
        chip,
        slabs,
        rows,
        tissue_mask.reshape(CZ * CX, YC),
        jnp.asarray(x_all),
        jnp.asarray(y_all),
    )


def on_device(
    patch_features, conv1_weight, conv1_bias, conv2_weight, conv2_bias, head_weight, tissue_mask
):
    params = pltpu.CompilerParams(vmem_limit_bytes=VMEM_LIMIT)
    patch = decode(
        patch_features, conv1_weight, conv1_bias, conv2_weight, conv2_bias, head_weight
    )
    pair = swap(patch, "chip")
    edge = pl.pallas_call(
        edge_kernel,
        out_shape=shape_of(EDGE, YC),
        in_specs=whole(1),
        out_specs=whole(1)[0],
        compiler_params=params,
        name="edge",
    )(pair)
    edges = swap(swap(edge, "x"), "chip")
    chip, send = pl.pallas_call(
        chip_kernel,
        out_shape=(shape_of(CHIP_ROWS * 32, YC), shape_of(SEND_ROWS * 32, YC)),
        in_specs=whole(2),
        out_specs=tuple(whole(2)),
        compiler_params=params,
        name="chip",
    )(pair, edges)
    slabs = swap(send, "slab")
    upper_core = lax.axis_index("gz") & 1
    row_at = jnp.where(upper_core == 1, SEND_ROWS * 32, (SEND_ROWS - 1) * 32)
    rows = swap(lax.dynamic_slice(slabs, (row_at, 0), (32, YC)), "chip")
    probability, vesselness = measure_tubes(chip, slabs, rows, tissue_mask)
    return (
        probability.reshape(CZ, CX, YC),
        vesselness.reshape(CZ, CX, YC),
    )


def solution(mesh):
    placed = (P(None, "gz", "xy", None), P(), P(), P(), P(), P(), P("gz", "xy", None))
    return jax.shard_map(
        on_device,
        mesh=mesh,
        in_specs=placed,
        out_specs=(P("gz", "xy", None), P("gz", "xy", None)),
        check_vma=False,
    )
```
